256 devices in a mesh: seq: 16 (over y, x), tensor: 8 (over z), dp: 2 (over core).
Axes of the slice: x: 4, y: 4, z: 8, core: 2. Of those that a mesh axis runs over, the one named last changes fastest.
Arguments:
- byte_states: bfloat16 [65536, 4096], P(('dp', 'seq'), 'tensor'), parts along dimension 0, may hold values from -6 to 6
- patch_spans: int32 [16384, 2], P(('dp', 'seq')), parts along dimension 0, may hold values from 0 to 32768, as said below
- doc_lengths: int32 [36], P('dp'), parts along dimension 0, may hold values from 1 to 2048, as said below
- norm_gain: float32 [4096], replicated, may hold values from 0.1 to 1.9
- w_query: bfloat16 [4096, 2048], P(None, 'tensor'), may hold values from -4 to 4
- w_key: bfloat16 [4096, 2048], P(None, 'tensor'), may hold values from -4 to 4
- w_value: bfloat16 [4096, 2048], P(None, 'tensor'), may hold values from -0.09375 to 0.09375
- w_out: bfloat16 [2048, 4096], P('tensor'), may hold values from -0.125 to 0.125
Outputs:
- attended_out: bfloat16 [16384, 4096], P(('dp', 'seq'), 'tensor'), parts along dimension 0
The draws below stay inside these ranges and needn't reach their ends.
There are 2 independent parts, one for each index of `dp`. The reference program is written for one: setup_inputs(seed, part) draws one part's arguments, and reference() takes and returns one part's arrays. A program takes and returns all parts, laid end to end along the dimension named above; an argument that names none is the same for every part. Nothing has to cross between parts.
Inputs may be any that keep to these rules, and one draw needn't show every extreme that they name: Patches are consecutive and cover all bytes: patch_spans[i, 1] == patch_spans[i + 1, 0], the first starts at 0, the last ends at 32768, each holds at least one byte. The patches of the k-th block of 512 patches lie within bytes k * 2048 - 512 to (k + 1) * 2048 + 512, and both ends of that margin are reached. `doc_lengths`: the lengths sum to 8192; exactly one document has 2048 patches.
All inputs are finite; a program needn't handle non-finite values.
Results may differ from the reference program's by a relative error of at most 0.018.
Values may be sent and summed in bfloat16 or wider, within the bound.
No kernel may reach another device: no remote copies, remote signals or barrier semaphores. Data moves between devices by JAX's collectives and lax.ppermute only.
A program may use at most 128 MiB of HBM per device.

```python
import jax
import jax.numpy as jnp
from jax import lax

D = 4096
HEADS = 16
HEAD_DIM = 128
P_DEV = 512
MOST = 2048
PATCHES = 8192
BYTES = 32768
DOCS = 18
N_TENSOR = 8


def draw_w_query(key, part):
    key = jax.random.fold_in(key, 21)
    own = jax.random.normal(key, (D, HEADS * HEAD_DIM), jnp.float32) / D ** 0.5
    return own.astype(jnp.bfloat16)


def draw_w_key(key, part):
    key = jax.random.fold_in(key, 22)
    own = jax.random.normal(key, (D, HEADS * HEAD_DIM), jnp.float32) / D ** 0.5
    return own.astype(jnp.bfloat16)


def draw_doc_lengths(key, part):
    key = jax.random.fold_in(key, 31)
    key_weights, key_place = jax.random.split(key)
    count = DOCS - 1
    extra = PATCHES - MOST - count
    weights = jax.random.randint(key_weights, (count,), 1, 9).astype(jnp.int32)
    marks = (extra * jnp.cumsum(weights) // jnp.sum(weights)).astype(jnp.int32)
    before = jnp.concatenate([jnp.zeros((1,), jnp.int32), marks[:-1]])
    others = (1 + marks - before).astype(jnp.int32)
    place = jax.random.randint(key_place, (), 0, DOCS).astype(jnp.int32)
    index = jnp.arange(DOCS, dtype=jnp.int32)
    lower = others[jnp.clip(index, 0, count - 1)]
    upper = others[jnp.clip(index - 1, 0, count - 1)]
    lengths = jnp.where(index < place, lower, jnp.where(index == place, MOST, upper))
    return lengths.astype(jnp.int32)


def draw_patch_spans(key, part):
    key = jax.random.fold_in(key, 11)
    shards = PATCHES // P_DEV
    block = 4 * P_DEV
    rim = P_DEV
    key_offsets, key_weights = jax.random.split(key)
    offsets = jax.random.randint(key_offsets, (shards + 1,), -rim, rim + 1)
    marker = jnp.arange(shards + 1, dtype=jnp.int32)
    offsets = jnp.where((marker == 0) | (marker == shards), 0, offsets)
    offsets = jnp.where(marker == 1, -rim, offsets)
    offsets = jnp.where(marker == 2, rim, offsets)
    bounds = marker * block + offsets
    spans = bounds[1:] - bounds[:-1]
    spare = spans - P_DEV
    weights = jax.random.randint(key_weights, (shards, P_DEV), 1, 9)
    before = jnp.cumsum(weights, axis=1) - weights
    whole = jnp.sum(weights, axis=1)
    starts = bounds[:-1, None] + spare[:, None] * before // whole[:, None] + jnp.arange(P_DEV, dtype=jnp.int32)[None, :]
    finish = jnp.concatenate([starts[:, 1:], bounds[1:, None]], axis=1)
    return jnp.stack([starts.reshape(-1), finish.reshape(-1)], axis=1).astype(jnp.int32)


def block_scale(own_key, extent, pieces, smallest, top_value):
    gain, own = 1.0, jax.random.fold_in(own_key, 6)
    for position, blocks in pieces:
        heights = jnp.exp(jax.random.uniform(jax.random.fold_in(own, position), (blocks,), jnp.float32, smallest / len(pieces), top_value / len(pieces)))
        gain = gain * jnp.repeat(heights, extent[position] // blocks).reshape([-1 if axis == position else 1 for axis in range(len(extent))])
    return gain


def bell_draw(rng, extent, scale, most, cuts=(), kind=jnp.bfloat16):
    entries = scale * jax.random.normal(rng, extent, jnp.float32)
    if cuts:
        entries = entries * block_scale(rng, extent, cuts, -0.22, 0.18)
    return jnp.clip(entries, -most, most).astype(kind)


def setup_inputs(seed: int = 0, part: int = 0) -> dict:
    key_of = jax.random.split(jax.random.key(seed), 9)
    own_keys = jax.random.split(jax.random.fold_in(key_of[8], part), 9)
    return {
        "byte_states": bell_draw(own_keys[0], (BYTES, D), 1.0, 6.0, ((0, 16), (1, 8))),
        "patch_spans": draw_patch_spans(jax.random.fold_in(jax.random.fold_in(key_of[8], part), 71), part),
        "doc_lengths": draw_doc_lengths(jax.random.fold_in(jax.random.fold_in(key_of[8], part), 71), part),
        "norm_gain": jnp.clip(1.0 + 0.18 * jax.random.normal(key_of[3], (D,), jnp.float32), 0.1, 1.9),
        "w_query": draw_w_query(jax.random.fold_in(key_of[8], 71), part),
        "w_key": draw_w_key(jax.random.fold_in(key_of[8], 71), part),
        "w_value": bell_draw(key_of[6], (D, HEADS * HEAD_DIM), D ** -0.5, 0.09375, ((1, 8),)),
        "w_out": bell_draw(key_of[7], (HEADS * HEAD_DIM, D), (HEADS * HEAD_DIM) ** -0.5, 0.125, ((0, 8),)),
    }


def doc_index(positions, doc_lengths):
    ends = jnp.cumsum(doc_lengths)
    return lax.optimization_barrier(jnp.sum((positions[:, None] >= ends[None, :]).astype(jnp.int32), axis=1))

def reference(byte_states, patch_spans, doc_lengths, norm_gain, w_query, w_key, w_value, w_out):
    starts = patch_spans[:, 0]
    finish = patch_spans[:, 1]
    marks = jnp.zeros((BYTES,), jnp.int32).at[starts].add(1)
    owner = (jnp.cumsum(marks) - 1).astype(jnp.int32)
    width = 512 if D % 512 == 0 else D
    columns = byte_states.reshape(BYTES, D // width, width).transpose(1, 0, 2)

    def pool_block(block):
        return jax.ops.segment_sum(block.astype(jnp.float32), owner, num_segments=PATCHES)
    sums = lax.map(pool_block, columns).transpose(1, 0, 2).reshape(PATCHES, D)
    counts = (finish - starts).astype(jnp.float32)
    pooled = (sums / counts[:, None]).astype(jnp.bfloat16)
    values_f = pooled.astype(jnp.float32)
    inverse = lax.rsqrt(lax.optimization_barrier(jnp.mean(values_f * values_f, axis=1, keepdims=True)) + 1e-05)
    normed = (values_f * inverse * norm_gain[None, :]).astype(jnp.bfloat16)
    query = jnp.dot(normed, w_query, preferred_element_type=jnp.float32).astype(jnp.bfloat16)
    keys = jnp.dot(normed, w_key, preferred_element_type=jnp.float32).astype(jnp.bfloat16)
    values = jnp.dot(normed, w_value, preferred_element_type=jnp.float32).astype(jnp.bfloat16)
    query = query.reshape(PATCHES, HEADS, HEAD_DIM).transpose(1, 0, 2)
    keys = keys.reshape(PATCHES, HEADS, HEAD_DIM).transpose(1, 0, 2)
    values = values.reshape(PATCHES, HEADS, HEAD_DIM).transpose(1, 0, 2)
    positions = jnp.arange(PATCHES, dtype=jnp.int32)
    doc = doc_index(positions, doc_lengths)
    allowed = (positions[None, :] <= positions[:, None]) & (doc[None, :] == doc[:, None])
    scale = 1.0 / HEAD_DIM ** 0.5

    def one_head(items):
        q_head, k_head, v_head = items
        scores = jnp.dot(q_head, k_head.T, preferred_element_type=jnp.float32) * scale
        scores = jnp.where(allowed, scores, -1e+30)
        top = lax.optimization_barrier(jnp.max(scores, axis=1, keepdims=True))
        weights = jnp.exp(scores - top) * allowed.astype(jnp.float32)
        total = lax.optimization_barrier(jnp.sum(weights, axis=1, keepdims=True))
        numer = jnp.dot(weights.astype(jnp.bfloat16), v_head, preferred_element_type=jnp.float32)
        return (numer / total).astype(jnp.bfloat16)
    attended = lax.map(one_head, (query, keys, values))
    attended = attended.transpose(1, 0, 2).reshape(PATCHES, HEADS * HEAD_DIM)
    group = HEADS // N_TENSOR * HEAD_DIM
    summed = jnp.zeros((PATCHES, D), jnp.float32)
    for index in range(N_TENSOR):
        partial_value = jnp.dot(attended[:, index * group:(index + 1) * group], w_out[index * group:(index + 1) * group, :], preferred_element_type=jnp.float32).astype(jnp.bfloat16)
        partial_value = lax.optimization_barrier(partial_value)
        summed = summed + partial_value.astype(jnp.float32)
    return summed.astype(jnp.bfloat16)
```

```python
import functools

import jax
import jax.numpy as jnp
from jax import lax
from jax.experimental import pallas as pl
from jax.experimental.pallas import tpu as pltpu
from jax.sharding import PartitionSpec as P

HEAD_DIM = 128
SIDE = 4
VMEM_LIMIT = 48 * 1024 * 1024
NEG = -1e30


def whole():
    return pl.BlockSpec(memory_space=pltpu.VMEM)


def params():
    return pltpu.CompilerParams(vmem_limit_bytes=VMEM_LIMIT)


def cost(flops, nbytes):
    return pl.CostEstimate(flops=flops, bytes_accessed=nbytes, transcendentals=0)


def member_of(first, rows, starts, finish):
    pos = first + lax.broadcasted_iota(jnp.int32, (starts.shape[0], rows), 1)
    return ((pos >= starts) & (pos < finish)).astype(jnp.float32).astype(jnp.bfloat16)


def pool_own_kernel(first_ref, bytes_ref, starts_ref, finish_ref, sums_ref):
    starts, finish = starts_ref[...], finish_ref[...]
    total = None
    step = 512
    for part in range(bytes_ref.shape[0] // step):
        member = member_of(first_ref[0] + part * step, step, starts, finish)
        value = jnp.dot(
            member, bytes_ref[part * step : (part + 1) * step, :], preferred_element_type=jnp.float32
        )
        total = value if total is None else total + value
    sums_ref[...] = total


def pool_rim_kernel(first_ref, before_ref, after_ref, sums_ref, starts_ref, finish_ref, *out_refs):
    half = out_refs[0].shape[0]
    rim = before_ref.shape[0]
    for index, out_ref in enumerate(out_refs):
        rows = slice(index * half, (index + 1) * half)
        starts, finish = starts_ref[rows, :], finish_ref[rows, :]
        total = sums_ref[rows, :]
        total += jnp.dot(
            member_of(first_ref[0], rim, starts, finish),
            before_ref[...],
            preferred_element_type=jnp.float32,
        )
        total += jnp.dot(
            member_of(first_ref[1], rim, starts, finish),
            after_ref[...],
            preferred_element_type=jnp.float32,
        )
        out_ref[...] = (total / (finish - starts).astype(jnp.float32)).astype(jnp.bfloat16)


def project_kernel(plan, fresh, close, index_ref, *refs):
    pieces = len(plan)
    slots = max(slot for _, slot in plan) + 1
    halves = sorted({half for half, _ in plan})
    refs = list(refs)
    x_refs = [refs.pop(0) for _ in range(pieces)]
    gain_refs = [refs.pop(0) for _ in range(slots)]
    w_refs = [[refs.pop(0) for _ in range(3)] for _ in range(slots)]
    sums = {}
    if not fresh:
        for half in halves:
            sums[half] = [refs.pop(0), refs.pop(0)]
    outs = refs
    for order, half in enumerate(halves):
        accum = [None, None, None]
        squares = None
        if not fresh:
            columns = w_refs[0][0].shape[1]
            accum = [sums[half][0][:, i * columns : (i + 1) * columns] for i in range(3)]
            squares = sums[half][1][...]
        for (own, slot), x_ref in zip(plan, x_refs):
            if own != half:
                continue
            values = x_ref[...].astype(jnp.float32)
            square = jnp.sum(values * values, axis=1, keepdims=True)
            square = jnp.broadcast_to(square, (square.shape[0], 128))
            squares = square if squares is None else squares + square
            scaled = (values * gain_refs[slot][0]).astype(jnp.bfloat16)
            for i in range(3):
                value = jnp.dot(scaled, w_refs[slot][i][...], preferred_element_type=jnp.float32)
                accum[i] = value if accum[i] is None else accum[i] + value
        columns = accum[0].shape[1]
        if close:
            features = close
            inverse = lax.rsqrt(squares[:, 0:1] / features + 1e-05)
            query_ref, pair_ref = outs[2 * order], outs[2 * order + 1]
            query_ref[...] = (accum[0] * inverse).astype(jnp.bfloat16)
            pair_ref[:, :columns] = (accum[1] * inverse).astype(jnp.bfloat16)
            pair_ref[:, columns:] = (accum[2] * inverse).astype(jnp.bfloat16)
        else:
            sum_ref, square_ref = outs[2 * order], outs[2 * order + 1]
            for i in range(3):
                sum_ref[:, i * columns : (i + 1) * columns] = accum[i]
            square_ref[...] = squares


def project(pieces, owners, gain, weights, sums=None, close=0):
    plan = tuple((half, slot) for half, slot, _ in pieces)
    halves = sorted({half for half, _ in plan})
    slots = max(slot for _, slot in plan) + 1
    rows, depth = pieces[0][2].shape
    columns = weights[0].shape[1]
    index = jnp.stack(owners).astype(jnp.int32)
    full = lambda shape: pl.BlockSpec(shape, lambda i, idx: (0,) * len(shape))
    operands = [x for _, _, x in pieces]
    specs = [full((rows, depth)) for _ in pieces]
    for slot in range(slots):
        operands.append(gain.reshape(-1, 1, depth))
        specs.append(pl.BlockSpec((1, 1, depth), lambda i, idx, slot=slot: (idx[slot], 0, 0)))
    for slot in range(slots):
        for w in weights:
            operands.append(w)
            specs.append(pl.BlockSpec((depth, columns), lambda i, idx, slot=slot: (idx[slot], 0)))
    if sums is not None:
        for half in halves:
            operands += list(sums[half])
            specs += [full((rows, 3 * columns)), full((rows, 128))]
    out_shape, out_specs = [], []
    for _ in halves:
        if close:
            out_shape += [
                jax.ShapeDtypeStruct((rows, columns), jnp.bfloat16),
                jax.ShapeDtypeStruct((rows, 2 * columns), jnp.bfloat16),
            ]
            out_specs += [full((rows, columns)), full((rows, 2 * columns))]
        else:
            out_shape += [
                jax.ShapeDtypeStruct((rows, 3 * columns), jnp.float32),
                jax.ShapeDtypeStruct((rows, 128), jnp.float32),
            ]
            out_specs += [full((rows, 3 * columns)), full((rows, 128))]
    outs = pl.pallas_call(
        functools.partial(project_kernel, plan, sums is None, close),
        grid_spec=pltpu.PrefetchScalarGridSpec(
            num_scalar_prefetch=1, grid=(1,), in_specs=specs, out_specs=out_specs
        ),
        out_shape=out_shape,
        compiler_params=params(),
        cost_estimate=cost(
            len(pieces) * 6 * rows * depth * columns, slots * 6 * depth * columns
        ),
        name="project",
    )(index, *operands)
    return {half: (outs[2 * i], outs[2 * i + 1]) for i, half in enumerate(halves)}


def attend_kernel(count, heads, scale, fresh, close, block_ref, *refs):
    refs = list(refs)
    q_refs = [refs.pop(0) for _ in range(2)]
    low_ref = refs.pop(0)
    pair_refs = [(refs.pop(0), refs.pop(0)) for _ in range(count)]
    if not fresh:
        old_top, old_total, old_accum = refs.pop(0), refs.pop(0), refs.pop(0)
    if close:
        out_refs = [refs.pop(0) for _ in range(2)]
        top_ref, total_ref, accum_ref = refs
    else:
        top_ref, total_ref, accum_ref = refs
    half = q_refs[0].shape[0]
    width = heads * HEAD_DIM
    if fresh:
        top_ref[...] = jnp.full(top_ref.shape, NEG, jnp.float32)
        total_ref[...] = jnp.zeros(total_ref.shape, jnp.float32)
        accum_ref[...] = jnp.zeros(accum_ref.shape, jnp.float32)
    else:
        top_ref[...] = old_top[...]
        total_ref[...] = old_total[...]
        accum_ref[...] = old_accum[...]
    here = block_ref[0]
    for slot in range(count):
        block = block_ref[1 + slot]

        @pl.when(block >= 0)
        def _(slot=slot, block=block):
            keys_of = pair_refs[slot]
            for qh in range(2):
                low = low_ref[qh * half : (qh + 1) * half, :]
                rows = slice(qh * half, (qh + 1) * half)
                query_pos = (2 * here + qh) * half + lax.broadcasted_iota(jnp.int32, (half, half), 0)
                for kh in range(2):
                    key_pos = (2 * block + kh) * half + lax.broadcasted_iota(
                        jnp.int32, (half, half), 1
                    )
                    allowed = (key_pos <= query_pos) & (key_pos >= low)
                    for head in range(heads):
                        cols = slice(head * HEAD_DIM, (head + 1) * HEAD_DIM)
                        values_cols = slice(width + head * HEAD_DIM, width + (head + 1) * HEAD_DIM)
                        scores = (
                            lax.dot_general(
                                q_refs[qh][:, cols],
                                keys_of[kh][:, cols],
                                (((1,), (1,)), ((), ())),
                                preferred_element_type=jnp.float32,
                            )
                            * scale
                        )
                        scores = jnp.where(allowed, scores, NEG)
                        top = top_ref[rows, cols]
                        new_top = jnp.maximum(top, jnp.max(scores, axis=1, keepdims=True))
                        fade = jnp.exp(top - new_top)
                        weights = jnp.where(allowed, jnp.exp(scores - new_top[:, 0:1]), 0.0)
                        total_ref[rows, cols] = total_ref[rows, cols] * fade + jnp.sum(
                            weights, axis=1, keepdims=True
                        )
                        update = jnp.dot(
                            weights.astype(jnp.bfloat16),
                            keys_of[kh][:, values_cols],
                            preferred_element_type=jnp.float32,
                        )
                        accum_ref[rows, cols] = accum_ref[rows, cols] * fade + update
                        top_ref[rows, cols] = new_top

    if close:
        for qh in range(2):
            rows = slice(qh * half, (qh + 1) * half)
            out_refs[qh][...] = (accum_ref[rows, :] / total_ref[rows, :]).astype(jnp.bfloat16)


def attend(queries, low, pairs, blocks, here, carry=None, close=False):
    rows = low.shape[0]
    half = rows // 2
    width = queries[0].shape[1]
    heads = width // HEAD_DIM
    index = jnp.stack([here] + list(blocks)).astype(jnp.int32)
    operands = list(queries) + [low]
    for pair in pairs:
        operands += list(pair)
    if carry is not None:
        operands += list(carry)
    state = [jax.ShapeDtypeStruct((rows, width), jnp.float32)] * 3
    scratch = []
    if close:
        out_shape = [jax.ShapeDtypeStruct((half, width), jnp.bfloat16)] * 2
        scratch = [pltpu.VMEM((rows, width), jnp.float32)] * 3
    else:
        out_shape = state
    flops = 4 * rows * rows * width * len(pairs)
    return pl.pallas_call(
        functools.partial(
            attend_kernel, len(pairs), heads, 1.0 / HEAD_DIM**0.5, carry is None, close
        ),
        in_specs=[pl.BlockSpec(memory_space=pltpu.SMEM)] + [whole()] * len(operands),
        out_specs=[whole()] * len(out_shape),
        out_shape=out_shape,
        scratch_shapes=scratch,
        compiler_params=params(),
        cost_estimate=cost(flops * 8, 4 * rows * width),
        name="attend",
    )(index, *operands)


def chips(move):
    pairs = []
    for y in range(SIDE):
        for x in range(SIDE):
            target = move(y, x)
            if target is not None:
                pairs.append((SIDE * y + x, SIDE * target[0] + target[1]))
    return pairs


def per_device(byte_states, patch_spans, doc_lengths, norm_gain, w_query, w_key, w_value, w_out):
    rank = lax.axis_index("seq")
    place = lax.axis_index("tensor")
    seq = lax.axis_size("seq")
    ring = lax.axis_size("tensor")
    byte_rows, depth = byte_states.shape
    rim = byte_rows // 4
    patch_rows = patch_spans.shape[0]
    half = patch_rows // 2
    column = rank % SIDE

    before = lax.ppermute(
        byte_states[byte_rows - rim :], "seq", [(i, i + 1) for i in range(seq - 1)]
    )
    after = lax.ppermute(byte_states[:rim], "seq", [(i + 1, i) for i in range(seq - 1)])
    starts = patch_spans[:, 0:1]
    finish = patch_spans[:, 1:2]
    first = rank * byte_rows
    smem = pl.BlockSpec(memory_space=pltpu.SMEM)
    sums = pl.pallas_call(
        pool_own_kernel,
        in_specs=[smem] + [whole()] * 3,
        out_specs=whole(),
        out_shape=jax.ShapeDtypeStruct((patch_rows, depth), jnp.float32),
        compiler_params=params(),
        cost_estimate=cost(4 * patch_rows * byte_rows * depth, 2 * byte_rows * depth),
        name="pool_own",
    )(jnp.stack([first]).astype(jnp.int32), byte_states, starts, finish)
    pooled = pl.pallas_call(
        pool_rim_kernel,
        in_specs=[smem] + [whole()] * 5,
        out_specs=[whole()] * 2,
        out_shape=[jax.ShapeDtypeStruct((half, depth), jnp.bfloat16)] * 2,
        compiler_params=params(),
        cost_estimate=cost(4 * patch_rows * rim * depth, 2 * rim * depth),
        name="pool_rim",
    )(
        jnp.stack([first - rim, first + byte_rows]).astype(jnp.int32),
        before,
        after,
        sums,
        starts,
        finish,
    )

    right = [(i, (i + 1) % ring) for i in range(ring)]
    left = [(j, i) for i, j in right]
    weights = (w_query, w_key, w_value)
    features = depth * ring
    going = [(pooled[0], pooled[0]), (pooled[1], pooled[1])]
    state = project(
        [(0, 0, pooled[0]), (1, 0, pooled[1])], [place], norm_gain, weights
    )
    for distance in range(1, ring // 2):
        going = [
            (lax.ppermute(a, "tensor", right), lax.ppermute(b, "tensor", left)) for a, b in going
        ]
        state = project(
            [(0, 0, going[0][0]), (0, 1, going[0][1]), (1, 0, going[1][0]), (1, 1, going[1][1])],
            [(place - distance) % ring, (place + distance) % ring],
            norm_gain,
            weights,
            state,
        )
    opposite = (place + ring // 2) % ring
    last = [
        lax.ppermute(going[0][0], "tensor", right),
        lax.ppermute(going[1][1], "tensor", left),
    ]
    queries, pairs = [], []
    for part in range(2):
        done = project(
            [(0, 0, last[part])], [opposite], norm_gain, weights, {0: state[part]}, features
        )
        queries.append(done[0][0])
        pairs.append(done[0][1])

    down = chips(lambda y, x: (y + 1, x) if y + 1 < SIDE else None)
    next_column = chips(lambda y, x: (y, x + 1) if x + 1 < SIDE else None)
    minus = chips(lambda y, x: (y, (x - 1) % SIDE))
    plus = chips(lambda y, x: (y, (x + 1) % SIDE) if x >= 1 else None)
    across = chips(lambda y, x: (y, x - 2) if x >= 2 else None)
    slots = {name: [] for name in ("above", "beside", "minus", "plus", "across")}
    for own in pairs:
        above = lax.ppermute(own, "seq", down)
        beside = lax.ppermute(own, "seq", next_column)
        slots["above"].append(above)
        slots["beside"].append(beside)
        slots["minus"].append(
            lax.ppermute(jnp.where(column == 0, own, above), "seq", minus)
        )
        slots["plus"].append(
            lax.ppermute(jnp.where(column == SIDE - 1, above, beside), "seq", plus)
        )
        slots["across"].append(lax.ppermute(above, "seq", across))
    back = lambda steps, here: jnp.where(here, rank - steps, -1)
    always = column >= 0
    blocks = {
        "above": back(4, always),
        "beside": back(1, column >= 1),
        "minus": back(3, always),
        "plus": jnp.where(column == 0, rank - 1, back(2, column >= 2)),
        "across": back(2, column < 2),
    }

    ends = jnp.cumsum(doc_lengths)
    positions = rank * patch_rows + jnp.arange(patch_rows, dtype=jnp.int32)
    low = jnp.max(jnp.where(ends[None, :] <= positions[:, None], ends[None, :], 0), axis=1)[:, None]

    carry = attend(queries, low, [pairs], [rank], rank)
    names = ("above", "beside")
    carry = attend(queries, low, [slots[n] for n in names], [blocks[n] for n in names], rank, carry)
    names = ("minus", "plus", "across")
    attended = attend(
        queries, low, [slots[n] for n in names], [blocks[n] for n in names], rank, carry, True
    )
    attended = jnp.concatenate(attended, axis=0)
    partial_value = jnp.dot(attended, w_out, preferred_element_type=jnp.float32)
    return lax.psum_scatter(
        partial_value.astype(jnp.bfloat16), "tensor", scatter_dimension=1, tiled=True
    )


def solution(mesh):
    in_specs = (
        P(("dp", "seq"), "tensor"),
        P(("dp", "seq"), None),
        P("dp"),
        P(),
        P(None, "tensor"),
        P(None, "tensor"),
        P(None, "tensor"),
        P("tensor", None),
    )
    out_specs = P(("dp", "seq"), "tensor")
    return jax.shard_map(
        per_device, mesh=mesh, in_specs=in_specs, out_specs=out_specs, check_vma=False
    )
```

```python
import functools

import jax
import jax.numpy as jnp
from jax import lax
from jax.experimental import pallas as pl
from jax.experimental.pallas import tpu as pltpu
from jax.sharding import PartitionSpec as P

HEAD_DIM = 128
SIDE = 4
VMEM_LIMIT = 16 * 1024 * 1024
NEG = -1e30
LOG2_E = 1.4426950408889634
F32 = jnp.float32
BF16 = jnp.bfloat16


def whole():
    return pl.BlockSpec(memory_space=pltpu.VMEM)


def scalars():
    return pl.BlockSpec(memory_space=pltpu.SMEM)


def params(limit=VMEM_LIMIT):
    return pltpu.CompilerParams(vmem_limit_bytes=limit)


def cost(flops, nbytes):
    return pl.CostEstimate(flops=flops, bytes_accessed=nbytes, transcendentals=0)


def shape(rows, columns, dtype=BF16):
    return jax.ShapeDtypeStruct((rows, columns), dtype)


def dot(a, b):
    return jnp.dot(a, b, preferred_element_type=F32)


def tie(value, *others):
    return lax.optimization_barrier((value, others))[0]


def member_of(first, rows, starts, finish):
    pos = first + lax.broadcasted_iota(jnp.int32, (starts.shape[0], rows), 1)
    return ((pos >= starts) & (pos < finish)).astype(F32).astype(BF16)


def pool_own_kernel(table_ref, bytes_ref, starts_ref, finish_ref, sums_ref, member_ref):
    starts, finish = starts_ref[...], finish_ref[...]
    rows = bytes_ref.shape[0]
    rim = rows // 4
    first = table_ref[0] * rows
    total = None
    for part in range(4):
        member = member_of(first + part * rim, rim, starts, finish)
        value = dot(member, bytes_ref[part * rim : (part + 1) * rim, :])
        total = value if total is None else total + value
    sums_ref[...] = total
    member_ref[:, :rim] = member_of(first - rim, rim, starts, finish)
    member_ref[:, rim:] = member_of(first + rows, rim, starts, finish)


def pool_rim_kernel(part, before_ref, after_ref, sums_ref, member_ref, starts_ref, finish_ref, out_ref):
    rim = before_ref.shape[0]
    width = out_ref.shape[1]
    cols = slice(part * width, (part + 1) * width)
    total = sums_ref[:, cols]
    total += dot(member_ref[:, :rim], before_ref[:, cols])
    total += dot(member_ref[:, rim:], after_ref[:, cols])
    out_ref[...] = (total / (finish_ref[...] - starts_ref[...]).astype(F32)).astype(BF16)


def project_kernel(plan, fresh, close, table_ref, gain_ref, q_ref, k_ref, v_ref, *refs):
    refs = list(refs)
    w_refs = [q_ref, k_ref, v_ref]
    x_refs = [refs.pop(0) for _ in plan]
    if fresh:
        sem = refs.pop()
        kept = refs[2:5]
        copies = [pltpu.make_async_copy(a, b, sem.at[i]) for i, (a, b) in enumerate(zip(w_refs, kept))]
        for copy in copies:
            copy.start()
        w_refs = kept
    else:
        old_sum, old_square = refs.pop(0), refs.pop(0)
    depth = x_refs[0].shape[1]
    columns = q_ref.shape[1]
    blocks = [2 * ((table_ref[1] + distance) % 8) + part for distance, part in plan]
    xs = []
    squares = None
    for ref, block in zip(x_refs, blocks):
        values = ref[...].astype(F32)
        square = values * values
        square = square[:, :128] + square[:, 128:]
        squares = square if squares is None else squares + square
        xs.append((values * gain_ref[block]).astype(BF16))
    if not fresh:
        squares = squares + old_square[...]
    if close:
        features, query_scale = close
        inverse = lax.rsqrt(jnp.sum(squares, axis=1, keepdims=True) / features + 1e-05)
    else:
        refs[1][...] = squares
    half = xs[0].shape[0] // 2
    for i, w_ref in enumerate(w_refs):
        cols = slice(i * columns, (i + 1) * columns)
        if fresh:
            copies[i].wait()
        total = None if fresh else old_sum[:, cols]
        for x, block in zip(xs, blocks):
            value = dot(x, w_ref[pl.ds(pl.multiple_of(block * depth, depth), depth), :])
            total = value if total is None else total + value
        if not close:
            refs[0][:, cols] = total
            continue
        total = total * (inverse * query_scale if i == 0 else inverse)
        for part in range(2):
            rows = slice(part * half, (part + 1) * half)
            if i == 0:
                refs[2 * part][...] = total[rows, :].astype(BF16)
            else:
                refs[2 * part + 1][:, (i - 1) * columns : i * columns] = total[rows, :].astype(BF16)


def project(table, pieces, gain, weights, sums=None, close=None):
    height, depth = pieces[0][2].shape
    columns = weights[0].shape[1]
    plan = tuple((distance, part) for distance, part, _ in pieces)
    rest = [x for _, _, x in pieces] + list(sums or ())
    fresh = sums is None
    scratch = []
    if close:
        out_shape = [shape(height // 2, columns), shape(height // 2, 2 * columns)] * 2
    else:
        out_shape = [shape(height, 3 * columns, F32), shape(height, 128, F32)]
    if fresh:
        out_shape += [shape(*w.shape) for w in weights]
        scratch = [pltpu.SemaphoreType.DMA((3,))]
    w_spec = pl.BlockSpec(memory_space=pltpu.HBM) if fresh else whole()
    return pl.pallas_call(
        functools.partial(project_kernel, plan, fresh, close),
        in_specs=[scalars(), whole()] + [w_spec] * 3 + [whole()] * len(rest),
        out_specs=[whole()] * len(out_shape),
        out_shape=out_shape,
        scratch_shapes=scratch,
        compiler_params=params(),
        cost_estimate=cost(len(plan) * 6 * height * depth * columns, 6 * depth * columns * len(plan)),
        name="project",
    )(table, gain, *weights, *rest)


def attend_kernel(steps, heads, own, fresh, close, table_ref, *refs):
    refs = list(refs)
    count = len(steps)
    q_refs = [refs.pop(0) for _ in range(2)]
    low_ref = refs.pop(0)
    pair_refs = [(refs.pop(0), refs.pop(0)) for _ in range(count)]
    olds = [] if fresh else [refs.pop(0) for _ in range(3)]
    out_refs = [refs.pop(0) for _ in range(2)] if close else []
    top_ref, total_ref, accum_ref = refs
    half = q_refs[0].shape[0]
    width = heads * HEAD_DIM
    if fresh:
        top_ref[...] = jnp.full(top_ref.shape, NEG, F32)
        total_ref[...] = jnp.zeros(total_ref.shape, F32)
        accum_ref[...] = jnp.zeros(accum_ref.shape, F32)
    else:
        for ref, old in zip((top_ref, total_ref, accum_ref), olds):
            ref[...] = old[...]
    here = table_ref[0]
    ones = jnp.ones((half, HEAD_DIM), BF16)

    def tile(slot, qh, block):
        low = low_ref[qh * half : (qh + 1) * half, :]
        rows = slice(qh * half, (qh + 1) * half)
        parts = (0,) if own and qh == 0 else (0, 1)
        allowed = {}
        for kh in parts:
            key_pos = (2 * block + kh) * half + lax.broadcasted_iota(jnp.int32, (half, half), 1)
            allowed[kh] = key_pos >= low
            if own and kh == qh:
                query_pos = (2 * here + qh) * half + lax.broadcasted_iota(jnp.int32, (half, half), 0)
                allowed[kh] = allowed[kh] & (key_pos <= query_pos)
        for head in range(heads):
            cols = slice(head * HEAD_DIM, (head + 1) * HEAD_DIM)
            value_cols = slice(width + head * HEAD_DIM, width + (head + 1) * HEAD_DIM)
            query = q_refs[qh][:, cols]
            scores = {}
            for kh in parts:
                value = lax.dot_general(
                    query,
                    pair_refs[slot][kh][:, cols],
                    (((1,), (1,)), ((), ())),
                    preferred_element_type=F32,
                )
                scores[kh] = jnp.where(allowed[kh], value, NEG)
            best = scores[0] if len(parts) == 1 else jnp.maximum(scores[0], scores[1])
            top = top_ref[rows, cols]
            new_top = jnp.maximum(top, jnp.max(best, axis=1, keepdims=True))
            fade = jnp.exp2(top - new_top)
            update = None
            for kh in parts:
                weights = jnp.exp2(scores[kh] - new_top[:, 0:1]).astype(BF16)
                values = jnp.concatenate([pair_refs[slot][kh][:, value_cols], ones], axis=1)
                value = dot(weights, values)
                update = value if update is None else update + value
            accum_ref[rows, cols] = accum_ref[rows, cols] * fade + update[:, :HEAD_DIM]
            total_ref[rows, cols] = total_ref[rows, cols] * fade + update[:, HEAD_DIM:]
            top_ref[rows, cols] = new_top

    for slot in range(count):
        block = here - steps[slot]
        for qh in range(2):
            if own:
                tile(slot, qh, block)
            else:
                pl.when((block >= 0) & ((block + 1) * 2 * half > table_ref[2 + qh]))(
                    functools.partial(tile, slot, qh, block)
                )
    for qh, ref in enumerate(out_refs):
        rows = slice(qh * half, (qh + 1) * half)
        ref[...] = (accum_ref[rows, :] / total_ref[rows, :]).astype(BF16)


def attend(table, queries, low, pairs, steps, carry=None, close=False):
    rows = low.shape[0]
    half = rows // 2
    width = queries[0].shape[1]
    heads = width // HEAD_DIM
    operands = list(queries) + [low]
    for pair in pairs:
        operands += list(pair)
    operands += list(carry or ())
    scratch = []
    if close:
        out_shape = [shape(half, width)] * 2
        scratch = [pltpu.VMEM((rows, width), F32)] * 3
    else:
        out_shape = [shape(rows, width, F32)] * 3
    fresh = carry is None
    return pl.pallas_call(
        functools.partial(attend_kernel, tuple(steps), heads, fresh, fresh, close),
        in_specs=[scalars()] + [whole()] * len(operands),
        out_specs=[whole()] * len(out_shape),
        out_shape=out_shape,
        scratch_shapes=scratch,
        compiler_params=params(),
        cost_estimate=cost(16 * rows * rows * width * len(pairs), 4 * rows * width),
        name="attend",
    )(table, *operands)


def share_kernel(given, distances, table_ref, attended_ref, w_ref, *refs):
    refs = list(refs)
    olds = [refs.pop(0) if has else None for has in given]
    width = w_ref.shape[1] // 8
    for order, (old, out_ref) in enumerate(zip(olds, refs)):
        first = pl.multiple_of((table_ref[1] + distances[order]) % 8 * width, width)
        value = dot(attended_ref[...], w_ref[:, pl.ds(first, width)])
        if old is not None:
            value = value + old[...].astype(F32)
        out_ref[...] = value.astype(BF16)


def share(table, attended, w_out, ring, targets, olds):
    rows = attended.shape[0]
    width = w_out.shape[1] // ring
    operands = [attended, w_out] + [old for old in olds if old is not None]
    return pl.pallas_call(
        functools.partial(share_kernel, tuple(old is not None for old in olds), tuple(d % ring for d in targets)),
        in_specs=[scalars()] + [whole()] * len(operands),
        out_specs=[whole()] * len(targets),
        out_shape=[shape(rows, width)] * len(targets),
        compiler_params=params(),
        cost_estimate=cost(2 * rows * width * attended.shape[1] * len(targets), 2 * rows * width * len(targets)),
        name="share",
    )(table, *operands)


def settle_kernel(table_ref, w_ref, *refs):
    out_ref = refs[-1]
    width = out_ref.shape[1]
    half = out_ref.shape[0] // 2
    first = pl.multiple_of(table_ref[1] * width, width)
    for part in range(2):
        attended_ref, a_ref, b_ref = refs[3 * part : 3 * part + 3]
        value = dot(attended_ref[...], w_ref[:, pl.ds(first, width)])
        value = value + a_ref[...].astype(F32) + b_ref[...].astype(F32)
        out_ref[part * half : (part + 1) * half, :] = value.astype(BF16)


def chips(move):
    pairs = []
    for y in range(SIDE):
        for x in range(SIDE):
            target = move(y, x)
            if target is not None:
                pairs.append((SIDE * y + x, SIDE * target[0] + target[1]))
    return pairs


def per_device(byte_states, patch_spans, doc_lengths, norm_gain, w_query, w_key, w_value, w_out):
    rank = lax.axis_index("seq")
    place = lax.axis_index("tensor")
    seq = lax.axis_size("seq")
    ring = lax.axis_size("tensor")
    byte_rows, depth = byte_states.shape
    rim = byte_rows // 4
    patch_rows = patch_spans.shape[0]
    half = patch_rows // 2
    column = rank % SIDE
    wide = depth // 2
    up = [(i, i + 1) for i in range(seq - 1)]
    down = [(j, i) for i, j in up]

    table = jnp.stack([rank, place]).astype(jnp.int32)

    last, first = byte_states[byte_rows - rim :], byte_states[:rim]
    before = lax.ppermute(last, "seq", up)
    after = lax.ppermute(first, "seq", down)
    starts = patch_spans[:, 0:1]
    finish = patch_spans[:, 1:2]
    ends = jnp.cumsum(doc_lengths)
    positions = rank * patch_rows + jnp.arange(patch_rows, dtype=jnp.int32)
    low = jnp.max(jnp.where(ends[None, :] <= positions[:, None], ends[None, :], 0), axis=1)[:, None]
    long_table = jnp.concatenate([table, low[0], low[half]])

    sums, member = pl.pallas_call(
        pool_own_kernel,
        in_specs=[scalars()] + [whole()] * 3,
        out_specs=[whole()] * 2,
        out_shape=[shape(patch_rows, depth, F32), shape(patch_rows, 2 * rim)],
        compiler_params=params(),
        cost_estimate=cost(4 * patch_rows * byte_rows * depth, 2 * byte_rows * depth),
        name="pool_own",
    )(table, byte_states, starts, finish)
    sums, low, long_table = lax.optimization_barrier((sums, low, long_table))
    pooled = [
        pl.pallas_call(
            functools.partial(pool_rim_kernel, part),
            in_specs=[whole()] * 6,
            out_specs=whole(),
            out_shape=shape(patch_rows, wide),
            compiler_params=params(),
            cost_estimate=cost(4 * patch_rows * rim * wide, 2 * rim * wide),
            name="pool_rim",
        )(before, after, sums, member, starts, finish)
        for part in range(2)
    ]

    right = [(i, (i + 1) % ring) for i in range(ring)]
    left = [(j, i) for i, j in right]
    gain = norm_gain.reshape(2 * ring, 1, wide)
    going = [(x, x) for x in pooled]
    states = [project(table, [(0, part, pooled[part]) for part in range(2)], gain, (w_query, w_key, w_value))]
    weights = states[0][2:]
    states[0] = states[0][:2]
    for distance in range(1, ring // 2):
        if distance > 1:
            going = [tuple(tie(x, states[distance - 2]) for x in pair) for pair in going]
        going = [
            (lax.ppermute(a, "tensor", right), lax.ppermute(b, "tensor", left)) for a, b in going
        ]
        pieces = []
        for part in range(2):
            pieces.append((ring - distance, part, going[part][0]))
            pieces.append((distance, part, going[part][1]))
        if distance < ring // 2 - 1:
            states.append(project(table, pieces, gain, weights, states[-1]))
    last = [
        lax.ppermute(tie(going[0][0], states[-1]), "tensor", right),
        lax.ppermute(tie(going[1][1], states[-1]), "tensor", left),
    ]
    pieces += [(ring // 2, part, last[part]) for part in range(2)]
    close = (float(depth * ring), LOG2_E / HEAD_DIM**0.5)
    done = project(table, pieces, gain, weights, states[-1], close)
    queries, pairs = done[0::2], done[1::2]

    lower = chips(lambda y, x: (y + 1, x) if y + 1 < SIDE else None)
    plus = chips(lambda y, x: (y, (x + 1) % SIDE))
    minus = chips(lambda y, x: (y, (x - 1) % SIDE))
    two = chips(lambda y, x: (y, (x + 2) % SIDE))
    slots = {4: [], 1: [], 3: [], 2: []}
    for own in pairs:
        above = lax.ppermute(own, "seq", lower)
        slots[4].append(above)
        slots[1].append(lax.ppermute(jnp.where(column == SIDE - 1, above, own), "seq", plus))
        slots[3].append(lax.ppermute(jnp.where(column == 0, own, above), "seq", minus))
        slots[2].append(lax.ppermute(jnp.where(column < 2, own, above), "seq", two))

    carry = attend(long_table, queries, low, [pairs], [0])
    for steps in ((4,), (1, 3), (2,)):
        carry = attend(
            long_table, queries, low, [slots[n] for n in steps], steps, carry, steps == (2,)
        )
    attended = carry

    far = ring // 2
    first = [(right, 1, left, -1), (left, -1, right, 1)]
    moving = []
    for part, (long, sign, short, other) in enumerate(first):
        a, b = share(table, attended[part], w_out, ring, [sign * far, other * (far - 1)], [None, None])
        moving.append([a, b])
    for distance in range(far, 0, -1):
        for part, (long, sign, short, other) in enumerate(first):
            a, b = moving[part]
            a = lax.ppermute(a, "tensor", long)
            if distance > 1:
                b = lax.ppermute(b, "tensor", short)
            if distance > 2:
                a, b = share(
                    table,
                    attended[part],
                    w_out,
                    ring,
                    [sign * (distance - 1), other * (distance - 2)],
                    [a, b],
                )
            elif distance == 2:
                (a,) = share(table, attended[part], w_out, ring, [sign], [a])
            moving[part] = [a, b]
    operands = [w_out]
    for part in range(2):
        operands += [attended[part]] + moving[part]
    return pl.pallas_call(
        settle_kernel,
        in_specs=[scalars()] + [whole()] * len(operands),
        out_specs=whole(),
        out_shape=shape(patch_rows, w_out.shape[1] // ring),
        compiler_params=params(),
        name="settle",
    )(table, *operands)


def solution(mesh):
    in_specs = (
        P(("dp", "seq"), "tensor"),
        P(("dp", "seq"), None),
        P("dp"),
        P(),
        P(None, "tensor"),
        P(None, "tensor"),
        P(None, "tensor"),
        P("tensor", None),
    )
    out_specs = P(("dp", "seq"), "tensor")
    return jax.shard_map(
        per_device, mesh=mesh, in_specs=in_specs, out_specs=out_specs, check_vma=False
    )
```

```python
import functools

import jax
import jax.numpy as jnp
from jax import lax
from jax.experimental import pallas as pl
from jax.experimental.pallas import tpu as pltpu
from jax.sharding import PartitionSpec as P

HEAD_DIM = 128
SIDE = 4
VMEM_LIMIT = 16 * 1024 * 1024
NEG = -1e30
LOG2_E = 1.4426950408889634
F32 = jnp.float32
BF16 = jnp.bfloat16


def whole():
    return pl.BlockSpec(memory_space=pltpu.VMEM)


def scalars():
    return pl.BlockSpec(memory_space=pltpu.SMEM)


def params(limit=VMEM_LIMIT):
    return pltpu.CompilerParams(vmem_limit_bytes=limit)


def cost(flops, nbytes):
    return pl.CostEstimate(flops=flops, bytes_accessed=nbytes, transcendentals=0)


def shape(rows, columns, dtype=BF16):
    return jax.ShapeDtypeStruct((rows, columns), dtype)


def dot(a, b):
    return jnp.dot(a, b, preferred_element_type=F32)


def tie(value, *others):
    return lax.optimization_barrier((value, others))[0]


def member_of(first, rows, starts, finish):
    pos = first + lax.broadcasted_iota(jnp.int32, (starts.shape[0], rows), 1)
    return ((pos >= starts) & (pos < finish)).astype(F32).astype(BF16)


def pool_own_kernel(table_ref, bytes_ref, starts_ref, finish_ref, sums_ref, member_ref):
    starts, finish = starts_ref[...], finish_ref[...]
    rows = bytes_ref.shape[0]
    rim = rows // 4
    first = table_ref[0] * rows
    total = None
    for part in range(4):
        member = member_of(first + part * rim, rim, starts, finish)
        value = dot(member, bytes_ref[part * rim : (part + 1) * rim, :])
        total = value if total is None else total + value
    sums_ref[...] = total
    member_ref[:, :rim] = member_of(first - rim, rim, starts, finish)
    member_ref[:, rim:] = member_of(first + rows, rim, starts, finish)


def pool_rim_kernel(part, before_ref, after_ref, sums_ref, member_ref, starts_ref, finish_ref, out_ref):
    rim = before_ref.shape[0]
    width = out_ref.shape[1]
    cols = slice(part * width, (part + 1) * width)
    total = sums_ref[:, cols]
    total += dot(member_ref[:, :rim], before_ref[:, cols])
    total += dot(member_ref[:, rim:], after_ref[:, cols])
    out_ref[...] = (total / (finish_ref[...] - starts_ref[...]).astype(F32)).astype(BF16)


def project_kernel(plan, fresh, close, table_ref, gain_ref, q_ref, k_ref, v_ref, *refs):
    refs = list(refs)
    w_refs = [q_ref, k_ref, v_ref]
    x_refs = [refs.pop(0) for _ in plan]
    if fresh:
        sem = refs.pop()
        kept = refs[2:5]
        copies = [pltpu.make_async_copy(a, b, sem.at[i]) for i, (a, b) in enumerate(zip(w_refs, kept))]
        for copy in copies:
            copy.start()
        w_refs = kept
    else:
        old_sum, old_square = refs.pop(0), refs.pop(0)
    depth = x_refs[0].shape[1]
    columns = q_ref.shape[1]
    blocks = [2 * ((table_ref[1] + distance) % 8) + part for distance, part in plan]
    xs = []
    squares = None
    for ref, block in zip(x_refs, blocks):
        values = ref[...].astype(F32)
        square = values * values
        square = square[:, :128] + square[:, 128:]
        squares = square if squares is None else squares + square
        xs.append((values * gain_ref[block]).astype(BF16))
    if not fresh:
        squares = squares + old_square[...]
    if close:
        features, query_scale = close
        inverse = lax.rsqrt(jnp.sum(squares, axis=1, keepdims=True) / features + 1e-05)
    else:
        refs[1][...] = squares
    half = xs[0].shape[0] // 2
    for i, w_ref in enumerate(w_refs):
        cols = slice(i * columns, (i + 1) * columns)
        if fresh:
            copies[i].wait()
        total = None if fresh else old_sum[:, cols]
        for x, block in zip(xs, blocks):
            value = dot(x, w_ref[pl.ds(pl.multiple_of(block * depth, depth), depth), :])
            total = value if total is None else total + value
        if not close:
            refs[0][:, cols] = total
            continue
        total = total * (inverse * query_scale if i == 0 else inverse)
        for part in range(2):
            rows = slice(part * half, (part + 1) * half)
            if i == 0:
                refs[2 * part][...] = total[rows, :].astype(BF16)
            else:
                refs[2 * part + 1][:, (i - 1) * columns : i * columns] = total[rows, :].astype(BF16)


def project(table, pieces, gain, weights, sums=None, close=None):
    height, depth = pieces[0][2].shape
    columns = weights[0].shape[1]
    plan = tuple((distance, part) for distance, part, _ in pieces)
    rest = [x for _, _, x in pieces] + list(sums or ())
    fresh = sums is None
    scratch = []
    if close:
        out_shape = [shape(height // 2, columns), shape(height // 2, 2 * columns)] * 2
    else:
        out_shape = [shape(height, 3 * columns, F32), shape(height, 128, F32)]
    if fresh:
        out_shape += [shape(*w.shape) for w in weights]
        scratch = [pltpu.SemaphoreType.DMA((3,))]
    w_spec = pl.BlockSpec(memory_space=pltpu.HBM) if fresh else whole()
    return pl.pallas_call(
        functools.partial(project_kernel, plan, fresh, close),
        in_specs=[scalars(), whole()] + [w_spec] * 3 + [whole()] * len(rest),
        out_specs=[whole()] * len(out_shape),
        out_shape=out_shape,
        scratch_shapes=scratch,
        compiler_params=params(),
        cost_estimate=cost(len(plan) * 6 * height * depth * columns, 6 * depth * columns * len(plan)),
        name="project",
    )(table, gain, *weights, *rest)


def attend_kernel(steps, heads, own, fresh, close, table_ref, *refs):
    refs = list(refs)
    count = len(steps)
    q_refs = [refs.pop(0) for _ in range(2)]
    low_ref = refs.pop(0)
    pair_refs = [(refs.pop(0), refs.pop(0)) for _ in range(count)]
    olds = [] if fresh else [refs.pop(0) for _ in range(3)]
    out_refs = [refs.pop(0) for _ in range(2)] if close else []
    top_ref, total_ref, accum_ref = refs
    half = q_refs[0].shape[0]
    width = heads * HEAD_DIM
    if fresh:
        top_ref[...] = jnp.full(top_ref.shape, NEG, F32)
        total_ref[...] = jnp.zeros(total_ref.shape, F32)
        accum_ref[...] = jnp.zeros(accum_ref.shape, F32)
    else:
        for ref, old in zip((top_ref, total_ref, accum_ref), olds):
            ref[...] = old[...]
    here = table_ref[0]
    ones = jnp.ones((half, HEAD_DIM), BF16)

    def tile(slot, qh, block):
        low = low_ref[qh * half : (qh + 1) * half, :]
        rows = slice(qh * half, (qh + 1) * half)
        parts = (0,) if own and qh == 0 else (0, 1)
        allowed = {}
        for kh in parts:
            key_pos = (2 * block + kh) * half + lax.broadcasted_iota(jnp.int32, (half, half), 1)
            allowed[kh] = key_pos >= low
            if own and kh == qh:
                query_pos = (2 * here + qh) * half + lax.broadcasted_iota(jnp.int32, (half, half), 0)
                allowed[kh] = allowed[kh] & (key_pos <= query_pos)
        for head in range(heads):
            cols = slice(head * HEAD_DIM, (head + 1) * HEAD_DIM)
            value_cols = slice(width + head * HEAD_DIM, width + (head + 1) * HEAD_DIM)
            query = q_refs[qh][:, cols]
            scores = {}
            for kh in parts:
                value = lax.dot_general(
                    query,
                    pair_refs[slot][kh][:, cols],
                    (((1,), (1,)), ((), ())),
                    preferred_element_type=F32,
                )
                scores[kh] = jnp.where(allowed[kh], value, NEG)
            best = scores[0] if len(parts) == 1 else jnp.maximum(scores[0], scores[1])
            top = top_ref[rows, cols]
            new_top = jnp.maximum(top, jnp.max(best, axis=1, keepdims=True))
            fade = jnp.exp2(top - new_top)
            update = None
            for kh in parts:
                weights = jnp.exp2(scores[kh] - new_top[:, 0:1]).astype(BF16)
                values = jnp.concatenate([pair_refs[slot][kh][:, value_cols], ones], axis=1)
                value = dot(weights, values)
                update = value if update is None else update + value
            accum_ref[rows, cols] = accum_ref[rows, cols] * fade + update[:, :HEAD_DIM]
            total_ref[rows, cols] = total_ref[rows, cols] * fade + update[:, HEAD_DIM:]
            top_ref[rows, cols] = new_top

    for slot in range(count):
        block = here - steps[slot]
        for qh in range(2):
            if own:
                tile(slot, qh, block)
            else:
                pl.when((block >= 0) & ((block + 1) * 2 * half > table_ref[2 + qh]))(
                    functools.partial(tile, slot, qh, block)
                )
    for qh, ref in enumerate(out_refs):
        rows = slice(qh * half, (qh + 1) * half)
        ref[...] = (accum_ref[rows, :] / total_ref[rows, :]).astype(BF16)


def attend(table, queries, low, pairs, steps, carry=None, close=False):
    rows = low.shape[0]
    half = rows // 2
    width = queries[0].shape[1]
    heads = width // HEAD_DIM
    operands = list(queries) + [low]
    for pair in pairs:
        operands += list(pair)
    operands += list(carry or ())
    scratch = []
    if close:
        out_shape = [shape(half, width)] * 2
        scratch = [pltpu.VMEM((rows, width), F32)] * 3
    else:
        out_shape = [shape(rows, width, F32)] * 3
    fresh = carry is None
    return pl.pallas_call(
        functools.partial(attend_kernel, tuple(steps), heads, fresh, fresh, close),
        in_specs=[scalars()] + [whole()] * len(operands),
        out_specs=[whole()] * len(out_shape),
        out_shape=out_shape,
        scratch_shapes=scratch,
        compiler_params=params(),
        cost_estimate=cost(16 * rows * rows * width * len(pairs), 4 * rows * width),
        name="attend",
    )(table, *operands)


def order_kernel(ranks, table_ref, mine_ref, other_ref, out_ref):
    width = mine_ref.shape[1]
    slice_rows = mine_ref.shape[0] // (8 * ranks)
    first_half = table_ref[4] == 0
    for rank in range(ranks):
        m = table_ref[0] ^ rank
        j = ((m >> 2) & 1) + 2 * ((m >> 3) & 1) + 4 * (m & 1) + 8 * ((m >> 1) & 1)
        for k in range(8):
            rows = pl.ds(pl.multiple_of((j * 8 + k) * slice_rows, slice_rows), slice_rows)
            target = slice((k * ranks + rank) * slice_rows, (k * ranks + rank + 1) * slice_rows)
            mine, other = mine_ref[rows, :], other_ref[rows, :]
            out_ref[target, :width] = jnp.where(first_half, mine, other)
            out_ref[target, width:] = jnp.where(first_half, other, mine)


def mix_kernel(plan, fresh, table_ref, w_ref, *refs):
    refs = list(refs)
    out_ref = refs.pop()
    x_refs = [refs.pop(0) for _ in plan]
    place = table_ref[1]
    for part in range(2):
        half, depth = x_refs[0].shape
        rows = slice(part * half, (part + 1) * half)
        total = None if fresh else refs[0][rows, :]
        for (distance, own), x_ref in zip(plan, x_refs):
            if own != part:
                continue
            q = place ^ ((place + distance) % 8)
            k = ((q >> 2) & 1) + 2 * ((q >> 1) & 1) + 4 * (q & 1)
            value = dot(x_ref[...], w_ref[pl.ds(pl.multiple_of(k * depth, depth), depth), :])
            total = value if total is None else total + value
        out_ref[rows, :] = total.astype(out_ref.dtype)


def mix(table, pieces, columns, total=None, dtype=F32):
    half, depth = pieces[0][2].shape
    width = columns.shape[1]
    operands = [columns] + [x for _, _, x in pieces] + ([] if total is None else [total])
    return pl.pallas_call(
        functools.partial(mix_kernel, tuple((d, p) for d, p, _ in pieces), total is None),
        in_specs=[scalars()] + [whole()] * len(operands),
        out_specs=whole(),
        out_shape=shape(2 * half, width, dtype),
        compiler_params=params(),
        cost_estimate=cost(2 * half * depth * width * len(pieces), 2 * half * width),
        name="mix",
    )(table, *operands)


def chips(move):
    pairs = []
    for y in range(SIDE):
        for x in range(SIDE):
            target = move(y, x)
            if target is not None:
                pairs.append((SIDE * y + x, SIDE * target[0] + target[1]))
    return pairs


def per_device(byte_states, patch_spans, doc_lengths, norm_gain, w_query, w_key, w_value, w_out):
    rank = lax.axis_index("seq")
    place = lax.axis_index("tensor")
    seq = lax.axis_size("seq")
    ring = lax.axis_size("tensor")
    byte_rows, depth = byte_states.shape
    rim = byte_rows // 4
    patch_rows = patch_spans.shape[0]
    half = patch_rows // 2
    column = rank % SIDE
    wide = depth // 2
    up = [(i, i + 1) for i in range(seq - 1)]
    down = [(j, i) for i, j in up]

    table = jnp.stack([rank, place]).astype(jnp.int32)

    last, first = byte_states[byte_rows - rim :], byte_states[:rim]
    before = lax.ppermute(last, "seq", up)
    after = lax.ppermute(first, "seq", down)

    slice_rows = w_out.shape[0] // seq
    columns = lax.dynamic_slice_in_dim(tie(w_out, last), rank * slice_rows, slice_rows, axis=0)
    for bit in (4, 2, 1):
        side = (place // bit) % 2
        wide_half = columns.shape[1] // 2
        keep = lax.dynamic_slice_in_dim(columns, side * wide_half, wide_half, axis=1)
        give = lax.dynamic_slice_in_dim(columns, (1 - side) * wide_half, wide_half, axis=1)
        got = lax.ppermute(give, "tensor", [(i, i ^ bit) for i in range(ring)])
        columns = jnp.concatenate([keep, got], axis=0)
    core = lax.axis_index("dp")
    columns = lax.dynamic_slice_in_dim(columns, core * (columns.shape[1] // 2), columns.shape[1] // 2, axis=1)
    double = lambda value, bit: jnp.concatenate(
        [value, lax.ppermute(value, "seq", [(i, i ^ bit) for i in range(seq)])], axis=0
    )

    starts = patch_spans[:, 0:1]
    finish = patch_spans[:, 1:2]
    ends = jnp.cumsum(doc_lengths)
    positions = rank * patch_rows + jnp.arange(patch_rows, dtype=jnp.int32)
    low = jnp.max(jnp.where(ends[None, :] <= positions[:, None], ends[None, :], 0), axis=1)[:, None]
    long_table = jnp.concatenate([table, low[0], low[half], lax.axis_index("dp").astype(jnp.int32)[None]])

    sums, member = pl.pallas_call(
        pool_own_kernel,
        in_specs=[scalars()] + [whole()] * 3,
        out_specs=[whole()] * 2,
        out_shape=[shape(patch_rows, depth, F32), shape(patch_rows, 2 * rim)],
        compiler_params=params(),
        cost_estimate=cost(4 * patch_rows * byte_rows * depth, 2 * byte_rows * depth),
        name="pool_own",
    )(table, byte_states, starts, finish)
    sums, low, long_table = lax.optimization_barrier((sums, low, long_table))
    pooled = [
        pl.pallas_call(
            functools.partial(pool_rim_kernel, part),
            in_specs=[whole()] * 6,
            out_specs=whole(),
            out_shape=shape(patch_rows, wide),
            compiler_params=params(),
            cost_estimate=cost(4 * patch_rows * rim * wide, 2 * rim * wide),
            name="pool_rim",
        )(before, after, sums, member, starts, finish)
        for part in range(2)
    ]

    right = [(i, (i + 1) % ring) for i in range(ring)]
    left = [(j, i) for i, j in right]
    gain = norm_gain.reshape(2 * ring, 1, wide)
    going = [(x, x) for x in pooled]
    states = [project(table, [(0, part, pooled[part]) for part in range(2)], gain, (w_query, w_key, w_value))]
    weights = states[0][2:]
    states[0] = states[0][:2]
    for distance in range(1, ring // 2):
        if distance > 1:
            going = [tuple(tie(x, states[distance - 2]) for x in pair) for pair in going]
            columns = double(tie(columns, states[distance - 2]), (4, 8)[distance - 2])
        going = [
            (lax.ppermute(a, "tensor", right), lax.ppermute(b, "tensor", left)) for a, b in going
        ]
        pieces = []
        for part in range(2):
            pieces.append((ring - distance, part, going[part][0]))
            pieces.append((distance, part, going[part][1]))
        if distance < ring // 2 - 1:
            states.append(project(table, pieces, gain, weights, states[-1]))
    last = [
        lax.ppermute(tie(going[0][0], states[-1]), "tensor", right),
        lax.ppermute(tie(going[1][1], states[-1]), "tensor", left),
    ]
    pieces += [(ring // 2, part, last[part]) for part in range(2)]
    columns = double(tie(columns, states[-1]), 1)
    close = (float(depth * ring), LOG2_E / HEAD_DIM**0.5)
    done = project(table, pieces, gain, weights, states[-1], close)
    queries, pairs = done[0::2], done[1::2]
    columns = double(tie(columns, pairs[1]), 2)

    lower = chips(lambda y, x: (y + 1, x) if y + 1 < SIDE else None)
    plus = chips(lambda y, x: (y, (x + 1) % SIDE))
    minus = chips(lambda y, x: (y, (x - 1) % SIDE))
    two = chips(lambda y, x: (y, (x + 2) % SIDE))
    slots = {4: [], 1: [], 3: [], 2: []}
    for own in pairs:
        above = lax.ppermute(own, "seq", lower)
        slots[4].append(above)
        slots[1].append(lax.ppermute(jnp.where(column == SIDE - 1, above, own), "seq", plus))
        slots[3].append(lax.ppermute(jnp.where(column == 0, own, above), "seq", minus))
        slots[2].append(lax.ppermute(jnp.where(column < 2, own, above), "seq", two))

    carry = attend(long_table, queries, low, [pairs], [0])
    columns = tie(columns, carry[0])
    others = lax.ppermute(columns, "dp", [(0, 1), (1, 0)])
    columns = pl.pallas_call(
        functools.partial(order_kernel, SIDE * SIDE),
        in_specs=[scalars()] + [whole()] * 2,
        out_specs=whole(),
        out_shape=shape(columns.shape[0], 2 * columns.shape[1]),
        compiler_params=params(),
        cost_estimate=cost(0, 8 * columns.shape[0] * columns.shape[1]),
        name="order",
    )(long_table, columns, others)
    for steps in ((4,), (1, 3), (2,)):
        carry = attend(
            long_table, queries, low, [slots[n] for n in steps], steps, carry, steps == (2,)
        )
    attended = carry

    going = [(x, x) for x in attended]
    pieces = [(0, part, attended[part]) for part in range(2)]
    for distance in range(1, ring // 2):
        going = [
            (lax.ppermute(a, "tensor", right), lax.ppermute(b, "tensor", left)) for a, b in going
        ]
        fresh = []
        for part in range(2):
            fresh.append((ring - distance, part, going[part][0]))
            fresh.append((distance, part, going[part][1]))
        if distance < ring // 2 - 1:
            pieces += fresh
    total = mix(long_table, pieces, columns)
    fresh += [
        (ring // 2, 0, lax.ppermute(tie(going[0][0], total), "tensor", right)),
        (ring // 2, 1, lax.ppermute(tie(going[1][1], total), "tensor", left)),
    ]
    return mix(long_table, fresh, columns, total, BF16)


def solution(mesh):
    in_specs = (
        P(("dp", "seq"), "tensor"),
        P(("dp", "seq"), None),
        P("dp"),
        P(),
        P(None, "tensor"),
        P(None, "tensor"),
        P(None, "tensor"),
        P("tensor", None),
    )
    out_specs = P(("dp", "seq"), "tensor")
    return jax.shard_map(
        per_device, mesh=mesh, in_specs=in_specs, out_specs=out_specs, check_vma=False
    )
```

```python
import functools

import jax
import jax.numpy as jnp
from jax import lax
from jax.experimental import pallas as pl
from jax.experimental.pallas import tpu as pltpu
from jax.sharding import PartitionSpec as P

HEAD_DIM = 128
SIDE = 4
VMEM_LIMIT = 16 * 1024 * 1024
NEG = -1e30
LOG2_E = 1.4426950408889634
F32 = jnp.float32
BF16 = jnp.bfloat16


def whole():
    return pl.BlockSpec(memory_space=pltpu.VMEM)


def scalars():
    return pl.BlockSpec(memory_space=pltpu.SMEM)


def params(limit=VMEM_LIMIT):
    return pltpu.CompilerParams(vmem_limit_bytes=limit)


def cost(flops, nbytes):
    return pl.CostEstimate(flops=flops, bytes_accessed=nbytes, transcendentals=0)


def shape(rows, columns, dtype=BF16):
    return jax.ShapeDtypeStruct((rows, columns), dtype)


def dot(a, b):
    return jnp.dot(a, b, preferred_element_type=F32)


def tie(value, *others):
    return lax.optimization_barrier((value, others))[0]


def member_of(first, rows, starts, finish):
    pos = first + lax.broadcasted_iota(jnp.int32, (starts.shape[0], rows), 1)
    return ((pos >= starts) & (pos < finish)).astype(F32).astype(BF16)


def pool_own_kernel(table_ref, bytes_ref, starts_ref, finish_ref, sums_ref, member_ref):
    starts, finish = starts_ref[...], finish_ref[...]
    rows = bytes_ref.shape[0]
    rim = rows // 4
    first = table_ref[0] * rows
    total = None
    for part in range(4):
        member = member_of(first + part * rim, rim, starts, finish)
        value = dot(member, bytes_ref[part * rim : (part + 1) * rim, :])
        total = value if total is None else total + value
    sums_ref[...] = total
    member_ref[:, :rim] = member_of(first - rim, rim, starts, finish)
    member_ref[:, rim:] = member_of(first + rows, rim, starts, finish)


def pool_rim_kernel(part, before_ref, after_ref, sums_ref, member_ref, starts_ref, finish_ref, out_ref):
    rim = before_ref.shape[0]
    width = out_ref.shape[1]
    cols = slice(part * width, (part + 1) * width)
    total = sums_ref[:, cols]
    total += dot(member_ref[:, :rim], before_ref[:, cols])
    total += dot(member_ref[:, rim:], after_ref[:, cols])
    out_ref[...] = (total / (finish_ref[...] - starts_ref[...]).astype(F32)).astype(BF16)


def project_kernel(plan, fresh, close, table_ref, gain_ref, q_ref, k_ref, v_ref, *refs):
    refs = list(refs)
    w_refs = [q_ref, k_ref, v_ref]
    x_refs = [refs.pop(0) for _ in plan]
    if fresh:
        sem = refs.pop()
        kept = refs[2:5]
        copies = [pltpu.make_async_copy(a, b, sem.at[i]) for i, (a, b) in enumerate(zip(w_refs, kept))]
        for copy in copies:
            copy.start()
        w_refs = kept
    else:
        old_sum, old_square = refs.pop(0), refs.pop(0)
    depth = x_refs[0].shape[1]
    columns = q_ref.shape[1]
    blocks = [2 * ((table_ref[1] + distance) % 8) + part for distance, part in plan]
    xs = []
    squares = None
    for ref, block in zip(x_refs, blocks):
        values = ref[...].astype(F32)
        square = values * values
        square = square[:, :128] + square[:, 128:]
        squares = square if squares is None else squares + square
        xs.append((values * gain_ref[block]).astype(BF16))
    if not fresh:
        squares = squares + old_square[...]
    if close:
        features, query_scale = close
        inverse = lax.rsqrt(jnp.sum(squares, axis=1, keepdims=True) / features + 1e-05)
    else:
        refs[1][...] = squares
    half = xs[0].shape[0] // 2
    for i, w_ref in enumerate(w_refs):
        cols = slice(i * columns, (i + 1) * columns)
        if fresh:
            copies[i].wait()
        total = None if fresh else old_sum[:, cols]
        for x, block in zip(xs, blocks):
            value = dot(x, w_ref[pl.ds(pl.multiple_of(block * depth, depth), depth), :])
            total = value if total is None else total + value
        if not close:
            refs[0][:, cols] = total
            continue
        total = total * (inverse * query_scale if i == 0 else inverse)
        for part in range(2):
            rows = slice(part * half, (part + 1) * half)
            if i == 0:
                refs[2 * part][...] = total[rows, :].astype(BF16)
            else:
                refs[2 * part + 1][:, (i - 1) * columns : i * columns] = total[rows, :].astype(BF16)


def project(table, pieces, gain, weights, sums=None, close=None):
    height, depth = pieces[0][2].shape
    columns = weights[0].shape[1]
    plan = tuple((distance, part) for distance, part, _ in pieces)
    rest = [x for _, _, x in pieces] + list(sums or ())
    fresh = sums is None
    scratch = []
    if close:
        out_shape = [shape(height // 2, columns), shape(height // 2, 2 * columns)] * 2
    else:
        out_shape = [shape(height, 3 * columns, F32), shape(height, 128, F32)]
    if fresh:
        out_shape += [shape(*w.shape) for w in weights]
        scratch = [pltpu.SemaphoreType.DMA((3,))]
    w_spec = pl.BlockSpec(memory_space=pltpu.HBM) if fresh else whole()
    return pl.pallas_call(
        functools.partial(project_kernel, plan, fresh, close),
        in_specs=[scalars(), whole()] + [w_spec] * 3 + [whole()] * len(rest),
        out_specs=[whole()] * len(out_shape),
        out_shape=out_shape,
        scratch_shapes=scratch,
        compiler_params=params(),
        cost_estimate=cost(len(plan) * 6 * height * depth * columns, 6 * depth * columns * len(plan)),
        name="project",
    )(table, gain, *weights, *rest)


def attend_kernel(steps, heads, own, fresh, close, table_ref, *refs):
    refs = list(refs)
    count = len(steps)
    q_refs = [refs.pop(0) for _ in range(2)]
    low_ref = refs.pop(0)
    pair_refs = [(refs.pop(0), refs.pop(0)) for _ in range(count)]
    olds = [] if fresh else [refs.pop(0) for _ in range(3)]
    out_refs = [refs.pop(0) for _ in range(2)] if close else []
    top_ref, total_ref, accum_ref = refs
    half = q_refs[0].shape[0]
    width = heads * HEAD_DIM
    if fresh:
        top_ref[...] = jnp.full(top_ref.shape, NEG, F32)
        total_ref[...] = jnp.zeros(total_ref.shape, F32)
        accum_ref[...] = jnp.zeros(accum_ref.shape, F32)
    else:
        for ref, old in zip((top_ref, total_ref, accum_ref), olds):
            ref[...] = old[...]
    here = table_ref[0]
    ones = jnp.ones((half, HEAD_DIM), BF16)

    def tile(slot, qh, block):
        low = low_ref[qh * half : (qh + 1) * half, :]
        rows = slice(qh * half, (qh + 1) * half)
        parts = (0,) if own and qh == 0 else (0, 1)
        allowed = {}
        for kh in parts:
            key_pos = (2 * block + kh) * half + lax.broadcasted_iota(jnp.int32, (half, half), 1)
            allowed[kh] = key_pos >= low
            if own and kh == qh:
                query_pos = (2 * here + qh) * half + lax.broadcasted_iota(jnp.int32, (half, half), 0)
                allowed[kh] = allowed[kh] & (key_pos <= query_pos)
        for head in range(heads):
            cols = slice(head * HEAD_DIM, (head + 1) * HEAD_DIM)
            value_cols = slice(width + head * HEAD_DIM, width + (head + 1) * HEAD_DIM)
            query = q_refs[qh][:, cols]
            scores = {}
            for kh in parts:
                value = lax.dot_general(
                    query,
                    pair_refs[slot][kh][:, cols],
                    (((1,), (1,)), ((), ())),
                    preferred_element_type=F32,
                )
                scores[kh] = jnp.where(allowed[kh], value, NEG)
            best = scores[0] if len(parts) == 1 else jnp.maximum(scores[0], scores[1])
            top = top_ref[rows, cols]
            new_top = jnp.maximum(top, jnp.max(best, axis=1, keepdims=True))
            fade = jnp.exp2(top - new_top)
            update = None
            for kh in parts:
                weights = jnp.exp2(scores[kh] - new_top[:, 0:1]).astype(BF16)
                values = jnp.concatenate([pair_refs[slot][kh][:, value_cols], ones], axis=1)
                value = dot(weights, values)
                update = value if update is None else update + value
            accum_ref[rows, cols] = accum_ref[rows, cols] * fade + update[:, :HEAD_DIM]
            total_ref[rows, cols] = total_ref[rows, cols] * fade + update[:, HEAD_DIM:]
            top_ref[rows, cols] = new_top

    for slot in range(count):
        block = here - steps[slot]
        for qh in range(2):
            if own:
                tile(slot, qh, block)
            else:
                pl.when((block >= 0) & ((block + 1) * 2 * half > table_ref[2 + qh]))(
                    functools.partial(tile, slot, qh, block)
                )
    for qh, ref in enumerate(out_refs):
        rows = slice(qh * half, (qh + 1) * half)
        ref[...] = (accum_ref[rows, :] / total_ref[rows, :]).astype(BF16)


def attend(table, queries, low, pairs, steps, carry=None, close=False):
    rows = low.shape[0]
    half = rows // 2
    width = queries[0].shape[1]
    heads = width // HEAD_DIM
    operands = list(queries) + [low]
    for pair in pairs:
        operands += list(pair)
    operands += list(carry or ())
    scratch = []
    if close:
        out_shape = [shape(half, width)] * 2
        scratch = [pltpu.VMEM((rows, width), F32)] * 3
    else:
        out_shape = [shape(rows, width, F32)] * 3
    fresh = carry is None
    return pl.pallas_call(
        functools.partial(attend_kernel, tuple(steps), heads, fresh, fresh, close),
        in_specs=[scalars()] + [whole()] * len(operands),
        out_specs=[whole()] * len(out_shape),
        out_shape=out_shape,
        scratch_shapes=scratch,
        compiler_params=params(),
        cost_estimate=cost(16 * rows * rows * width * len(pairs), 4 * rows * width),
        name="attend",
    )(table, *operands)


def join_kernel(a_ref, b_ref, out_ref):
    rows = a_ref.shape[0]
    out_ref[:rows, :] = a_ref[...]
    out_ref[rows:, :] = b_ref[...]


def join(a, b):
    return pl.pallas_call(
        join_kernel,
        in_specs=[whole()] * 2,
        out_specs=whole(),
        out_shape=shape(2 * a.shape[0], a.shape[1]),
        compiler_params=params(),
        cost_estimate=cost(0, 8 * a.shape[0] * a.shape[1]),
        name="join",
    )(a, b)


def slice_of(rank):
    return ((rank >> 2) & 1) + 2 * ((rank >> 3) & 1) + 4 * (rank & 1)


def order_kernel(ranks, table_ref, mine_ref, other_ref, out_ref):
    width = mine_ref.shape[1]
    slice_rows = mine_ref.shape[0] // (8 * ranks)
    first_half = table_ref[4] == 0
    mine_at = slice_of(table_ref[0])
    for rank in range(ranks):
        j = mine_at ^ rank
        for k in range(8):
            rows = pl.ds(pl.multiple_of((j * 8 + k) * slice_rows, slice_rows), slice_rows)
            target = slice((k * ranks + rank) * slice_rows, (k * ranks + rank + 1) * slice_rows)
            mine, other = mine_ref[rows, :], other_ref[rows, :]
            out_ref[target, :width] = jnp.where(first_half, mine, other)
            out_ref[target, width:] = jnp.where(first_half, other, mine)


def mix_kernel(plan, fresh, table_ref, w_ref, *refs):
    refs = list(refs)
    out_ref = refs.pop()
    x_refs = [refs.pop(0) for _ in plan]
    place = table_ref[1]
    for part in range(2):
        half, depth = x_refs[0].shape
        rows = slice(part * half, (part + 1) * half)
        total = None if fresh else refs[0][rows, :]
        for (distance, own), x_ref in zip(plan, x_refs):
            if own != part:
                continue
            q = place ^ ((place + distance) % 8)
            k = ((q >> 2) & 1) + 2 * ((q >> 1) & 1) + 4 * (q & 1)
            value = dot(x_ref[...], w_ref[pl.ds(pl.multiple_of(k * depth, depth), depth), :])
            total = value if total is None else total + value
        out_ref[rows, :] = total.astype(out_ref.dtype)


def mix(table, pieces, columns, total=None, dtype=F32):
    half, depth = pieces[0][2].shape
    width = columns.shape[1]
    operands = [columns] + [x for _, _, x in pieces] + ([] if total is None else [total])
    return pl.pallas_call(
        functools.partial(mix_kernel, tuple((d, p) for d, p, _ in pieces), total is None),
        in_specs=[scalars()] + [whole()] * len(operands),
        out_specs=whole(),
        out_shape=shape(2 * half, width, dtype),
        compiler_params=params(),
        cost_estimate=cost(2 * half * depth * width * len(pieces), 2 * half * width),
        name="mix",
    )(table, *operands)


def chips(move):
    pairs = []
    for y in range(SIDE):
        for x in range(SIDE):
            target = move(y, x)
            if target is not None:
                pairs.append((SIDE * y + x, SIDE * target[0] + target[1]))
    return pairs


def per_device(byte_states, patch_spans, doc_lengths, norm_gain, w_query, w_key, w_value, w_out):
    rank = lax.axis_index("seq")
    place = lax.axis_index("tensor")
    seq = lax.axis_size("seq")
    ring = lax.axis_size("tensor")
    byte_rows, depth = byte_states.shape
    rim = byte_rows // 4
    patch_rows = patch_spans.shape[0]
    half = patch_rows // 2
    column = rank % SIDE
    wide = depth // 2
    up = [(i, i + 1) for i in range(seq - 1)]
    down = [(j, i) for i, j in up]

    table = jnp.stack([rank, place]).astype(jnp.int32)

    last, first = byte_states[byte_rows - rim :], byte_states[:rim]
    before = lax.ppermute(last, "seq", up)
    after = lax.ppermute(first, "seq", down)

    slices = 2 * SIDE
    slice_rows = w_out.shape[0] // slices

    def cut(value, bit):
        side = (place // bit) % 2
        wide_half = value.shape[1] // 2
        keep = lax.dynamic_slice_in_dim(value, side * wide_half, wide_half, axis=1)
        give = lax.dynamic_slice_in_dim(value, (1 - side) * wide_half, wide_half, axis=1)
        return keep, give

    def trade(keep, give, bit):
        got = lax.ppermute(give, "tensor", [(i, i ^ bit) for i in range(ring)])
        return jnp.concatenate([keep, got], axis=0)

    columns = lax.dynamic_slice_in_dim(w_out, slice_of(rank) * slice_rows, slice_rows, axis=0)
    for bit in (4, 2):
        columns = trade(*cut(columns, bit), bit)
    keep, give = cut(columns, 1)
    double = lambda value, bit: join(
        value, lax.ppermute(value, "seq", [(i, i ^ bit) for i in range(seq)])
    )

    starts = patch_spans[:, 0:1]
    finish = patch_spans[:, 1:2]
    ends = jnp.cumsum(doc_lengths)
    positions = rank * patch_rows + jnp.arange(patch_rows, dtype=jnp.int32)
    low = jnp.max(jnp.where(ends[None, :] <= positions[:, None], ends[None, :], 0), axis=1)[:, None]
    long_table = jnp.concatenate([table, low[0], low[half], lax.axis_index("dp").astype(jnp.int32)[None]])

    sums, member = pl.pallas_call(
        pool_own_kernel,
        in_specs=[scalars()] + [whole()] * 3,
        out_specs=[whole()] * 2,
        out_shape=[shape(patch_rows, depth, F32), shape(patch_rows, 2 * rim)],
        compiler_params=params(),
        cost_estimate=cost(4 * patch_rows * byte_rows * depth, 2 * byte_rows * depth),
        name="pool_own",
    )(table, byte_states, starts, finish)
    sums, low, long_table, keep, give = lax.optimization_barrier((sums, low, long_table, keep, give))
    columns = trade(keep, give, 1)
    core = lax.axis_index("dp")
    columns = lax.dynamic_slice_in_dim(columns, core * (columns.shape[1] // 2), columns.shape[1] // 2, axis=1)
    pooled = [
        pl.pallas_call(
            functools.partial(pool_rim_kernel, part),
            in_specs=[whole()] * 6,
            out_specs=whole(),
            out_shape=shape(patch_rows, wide),
            compiler_params=params(),
            cost_estimate=cost(4 * patch_rows * rim * wide, 2 * rim * wide),
            name="pool_rim",
        )(before, after, sums, member, starts, finish)
        for part in range(2)
    ]

    right = [(i, (i + 1) % ring) for i in range(ring)]
    left = [(j, i) for i, j in right]
    gain = norm_gain.reshape(2 * ring, 1, wide)
    going = [(x, x) for x in pooled]
    states = [project(table, [(0, part, pooled[part]) for part in range(2)], gain, (w_query, w_key, w_value))]
    weights = states[0][2:]
    states[0] = states[0][:2]
    for distance in range(1, ring // 2):
        if distance > 1:
            early = (states[distance - 2],) if distance == 2 else (states[distance - 2], columns)
            going = [tuple(tie(x, *early) for x in pair) for pair in going]
            columns = double(tie(columns, states[distance - 2]), (4, 8)[distance - 2])
        going = [
            (lax.ppermute(a, "tensor", right), lax.ppermute(b, "tensor", left)) for a, b in going
        ]
        pieces = []
        for part in range(2):
            pieces.append((ring - distance, part, going[part][0]))
            pieces.append((distance, part, going[part][1]))
        if distance < ring // 2 - 1:
            states.append(project(table, pieces, gain, weights, states[-1]))
    last = [
        lax.ppermute(tie(going[0][0], states[-1], columns), "tensor", right),
        lax.ppermute(tie(going[1][1], states[-1], columns), "tensor", left),
    ]
    pieces += [(ring // 2, part, last[part]) for part in range(2)]
    columns = double(tie(columns, states[-1]), 1)
    close = (float(depth * ring), LOG2_E / HEAD_DIM**0.5)
    done = project(table, pieces, gain, weights, states[-1], close)
    queries, pairs = done[0::2], done[1::2]

    lower = chips(lambda y, x: (y + 1, x) if y + 1 < SIDE else None)
    plus = chips(lambda y, x: (y, (x + 1) % SIDE))
    minus = chips(lambda y, x: (y, (x - 1) % SIDE))
    two = chips(lambda y, x: (y, (x + 2) % SIDE))
    slots = {4: [], 1: [], 3: [], 2: []}
    for own in pairs:
        above = lax.ppermute(own, "seq", lower)
        slots[4].append(above)
        slots[1].append(lax.ppermute(jnp.where(column == SIDE - 1, above, own), "seq", plus))
        slots[3].append(lax.ppermute(jnp.where(column == 0, own, above), "seq", minus))
        slots[2].append(lax.ppermute(jnp.where(column < 2, own, above), "seq", two))

    carry = attend(long_table, queries, low, [pairs], [0])
    columns = tie(columns, carry[0])
    others = lax.ppermute(columns, "dp", [(0, 1), (1, 0)])
    columns = pl.pallas_call(
        functools.partial(order_kernel, slices),
        in_specs=[scalars()] + [whole()] * 2,
        out_specs=whole(),
        out_shape=shape(columns.shape[0], 2 * columns.shape[1]),
        compiler_params=params(),
        cost_estimate=cost(0, 8 * columns.shape[0] * columns.shape[1]),
        name="order",
    )(long_table, columns, others)
    for steps in ((4,), (1, 3), (2,)):
        carry = attend(
            long_table, queries, low, [slots[n] for n in steps], steps, carry, steps == (2,)
        )
    attended = carry

    going = [(x, x) for x in attended]
    pieces = [(0, part, attended[part]) for part in range(2)]
    for distance in range(1, ring // 2):
        going = [
            (lax.ppermute(a, "tensor", right), lax.ppermute(b, "tensor", left)) for a, b in going
        ]
        fresh = []
        for part in range(2):
            fresh.append((ring - distance, part, going[part][0]))
            fresh.append((distance, part, going[part][1]))
        if distance < ring // 2 - 1:
            pieces += fresh
    total = mix(long_table, pieces, columns)
    fresh += [
        (ring // 2, 0, lax.ppermute(tie(going[0][0], total), "tensor", right)),
        (ring // 2, 1, lax.ppermute(tie(going[1][1], total), "tensor", left)),
    ]
    return mix(long_table, fresh, columns, total, BF16)


def solution(mesh):
    in_specs = (
        P(("dp", "seq"), "tensor"),
        P(("dp", "seq"), None),
        P("dp"),
        P(),
        P(None, "tensor"),
        P(None, "tensor"),
        P(None, "tensor"),
        P("tensor", None),
    )
    out_specs = P(("dp", "seq"), "tensor")
    return jax.shard_map(
        per_device, mesh=mesh, in_specs=in_specs, out_specs=out_specs, check_vma=False
    )
```

```python
import functools

import jax
import jax.numpy as jnp
from jax import lax
from jax.experimental import pallas as pl
from jax.experimental.pallas import tpu as pltpu
from jax.sharding import PartitionSpec as P

HEAD_DIM = 128
SIDE = 4
VMEM_LIMIT = 16 * 1024 * 1024
FIRST_LIMIT = 44 * 1024 * 1024
NEG = -1e30
LOG2_E = 1.4426950408889634
F32 = jnp.float32
BF16 = jnp.bfloat16


def whole():
    return pl.BlockSpec(memory_space=pltpu.VMEM)


def scalars():
    return pl.BlockSpec(memory_space=pltpu.SMEM)


def params(limit=VMEM_LIMIT):
    return pltpu.CompilerParams(vmem_limit_bytes=limit)


def cost(flops, nbytes):
    return pl.CostEstimate(flops=flops, bytes_accessed=nbytes, transcendentals=0)


def shape(rows, columns, dtype=BF16):
    return jax.ShapeDtypeStruct((rows, columns), dtype)


def dot(a, b):
    return jnp.dot(a, b, preferred_element_type=F32)


def tie(value, *others):
    return lax.optimization_barrier((value, others))[0]


def member_of(first, rows, starts, finish):
    pos = first + lax.broadcasted_iota(jnp.int32, (starts.shape[0], rows), 1)
    return ((pos >= starts) & (pos < finish)).astype(F32).astype(BF16)


def pool_own_kernel(table_ref, bytes_ref, starts_ref, finish_ref, sums_ref, member_ref):
    starts, finish = starts_ref[...], finish_ref[...]
    rows = bytes_ref.shape[0]
    rim = rows // 4
    first = table_ref[0] * rows
    total = None
    for part in range(4):
        member = member_of(first + part * rim, rim, starts, finish)
        value = dot(member, bytes_ref[part * rim : (part + 1) * rim, :])
        total = value if total is None else total + value
    sums_ref[...] = total
    member_ref[:, :rim] = member_of(first - rim, rim, starts, finish)
    member_ref[:, rim:] = member_of(first + rows, rim, starts, finish)


def pool_rim_kernel(part, before_ref, after_ref, sums_ref, member_ref, starts_ref, finish_ref, out_ref):
    rim = before_ref.shape[0]
    width = out_ref.shape[1]
    cols = slice(part * width, (part + 1) * width)
    total = sums_ref[:, cols]
    total += dot(member_ref[:, :rim], before_ref[:, cols])
    total += dot(member_ref[:, rim:], after_ref[:, cols])
    out_ref[...] = (total / (finish_ref[...] - starts_ref[...]).astype(F32)).astype(BF16)


def project_kernel(plan, fresh, close, table_ref, gain_ref, q_ref, k_ref, v_ref, *refs):
    refs = list(refs)
    w_refs = [q_ref, k_ref, v_ref]
    x_refs = [refs.pop(0) for _ in plan]
    if fresh:
        sem = refs.pop()
        kept = refs[2:5]
        copies = [pltpu.make_async_copy(a, b, sem.at[i]) for i, (a, b) in enumerate(zip(w_refs, kept))]
        for copy in copies:
            copy.start()
        w_refs = kept
    else:
        old_sum, old_square = refs.pop(0), refs.pop(0)
    depth = x_refs[0].shape[1]
    columns = q_ref.shape[1]
    blocks = [2 * ((table_ref[1] + distance) % 8) + part for distance, part in plan]
    xs = []
    squares = None
    for ref, block in zip(x_refs, blocks):
        values = ref[...].astype(F32)
        square = values * values
        square = square[:, :128] + square[:, 128:]
        squares = square if squares is None else squares + square
        xs.append((values * gain_ref[block]).astype(BF16))
    if not fresh:
        squares = squares + old_square[...]
    if close:
        features, query_scale = close
        inverse = lax.rsqrt(jnp.sum(squares, axis=1, keepdims=True) / features + 1e-05)
    else:
        refs[1][...] = squares
    half = xs[0].shape[0] // 2
    for i, w_ref in enumerate(w_refs):
        cols = slice(i * columns, (i + 1) * columns)
        if fresh:
            copies[i].wait()
        total = None if fresh else old_sum[:, cols]
        for x, block in zip(xs, blocks):
            value = dot(x, w_ref[pl.ds(pl.multiple_of(block * depth, depth), depth), :])
            total = value if total is None else total + value
        if not close:
            refs[0][:, cols] = total
            continue
        total = total * (inverse * query_scale if i == 0 else inverse)
        for part in range(2):
            rows = slice(part * half, (part + 1) * half)
            if i == 0:
                refs[2 * part][...] = total[rows, :].astype(BF16)
            else:
                refs[2 * part + 1][:, (i - 1) * columns : i * columns] = total[rows, :].astype(BF16)


def project(table, pieces, gain, weights, sums=None, close=None):
    height, depth = pieces[0][2].shape
    columns = weights[0].shape[1]
    plan = tuple((distance, part) for distance, part, _ in pieces)
    rest = [x for _, _, x in pieces] + list(sums or ())
    fresh = sums is None
    scratch = []
    if close:
        out_shape = [shape(height // 2, columns), shape(height // 2, 2 * columns)] * 2
    else:
        out_shape = [shape(height, 3 * columns, F32), shape(height, 128, F32)]
    if fresh:
        out_shape += [shape(*w.shape) for w in weights]
        scratch = [pltpu.SemaphoreType.DMA((3,))]
    w_spec = pl.BlockSpec(memory_space=pltpu.HBM) if fresh else whole()
    return pl.pallas_call(
        functools.partial(project_kernel, plan, fresh, close),
        in_specs=[scalars(), whole()] + [w_spec] * 3 + [whole()] * len(rest),
        out_specs=[whole()] * len(out_shape),
        out_shape=out_shape,
        scratch_shapes=scratch,
        compiler_params=params(FIRST_LIMIT if fresh else VMEM_LIMIT),
        cost_estimate=cost(len(plan) * 6 * height * depth * columns, 6 * depth * columns * len(plan)),
        name="project",
    )(table, gain, *weights, *rest)


def attend_kernel(steps, heads, own, fresh, close, table_ref, *refs):
    refs = list(refs)
    count = len(steps)
    q_refs = [refs.pop(0) for _ in range(2)]
    low_ref = refs.pop(0)
    pair_refs = [(refs.pop(0), refs.pop(0)) for _ in range(count)]
    olds = [] if fresh else [refs.pop(0) for _ in range(3)]
    out_refs = [refs.pop(0) for _ in range(2)] if close else []
    top_ref, total_ref, accum_ref = refs
    half = q_refs[0].shape[0]
    width = heads * HEAD_DIM
    if fresh:
        top_ref[...] = jnp.full(top_ref.shape, NEG, F32)
        total_ref[...] = jnp.zeros(total_ref.shape, F32)
        accum_ref[...] = jnp.zeros(accum_ref.shape, F32)
    else:
        for ref, old in zip((top_ref, total_ref, accum_ref), olds):
            ref[...] = old[...]
    here = table_ref[0]
    ones = jnp.ones((half, HEAD_DIM), BF16)

    def tile(slot, qh, block):
        low = low_ref[qh * half : (qh + 1) * half, :]
        rows = slice(qh * half, (qh + 1) * half)
        parts = (0,) if own and qh == 0 else (0, 1)
        allowed = {}
        for kh in parts:
            key_pos = (2 * block + kh) * half + lax.broadcasted_iota(jnp.int32, (half, half), 1)
            allowed[kh] = key_pos >= low
            if own and kh == qh:
                query_pos = (2 * here + qh) * half + lax.broadcasted_iota(jnp.int32, (half, half), 0)
                allowed[kh] = allowed[kh] & (key_pos <= query_pos)
        for head in range(heads):
            cols = slice(head * HEAD_DIM, (head + 1) * HEAD_DIM)
            value_cols = slice(width + head * HEAD_DIM, width + (head + 1) * HEAD_DIM)
            query = q_refs[qh][:, cols]
            scores = {}
            for kh in parts:
                value = lax.dot_general(
                    query,
                    pair_refs[slot][kh][:, cols],
                    (((1,), (1,)), ((), ())),
                    preferred_element_type=F32,
                )
                scores[kh] = jnp.where(allowed[kh], value, NEG)
            best = scores[0] if len(parts) == 1 else jnp.maximum(scores[0], scores[1])
            top = top_ref[rows, cols]
            new_top = jnp.maximum(top, jnp.max(best, axis=1, keepdims=True))
            fade = jnp.exp2(top - new_top)
            update = None
            for kh in parts:
                weights = jnp.exp2(scores[kh] - new_top[:, 0:1]).astype(BF16)
                values = jnp.concatenate([pair_refs[slot][kh][:, value_cols], ones], axis=1)
                value = dot(weights, values)
                update = value if update is None else update + value
            accum_ref[rows, cols] = accum_ref[rows, cols] * fade + update[:, :HEAD_DIM]
            total_ref[rows, cols] = total_ref[rows, cols] * fade + update[:, HEAD_DIM:]
            top_ref[rows, cols] = new_top

    for slot in range(count):
        block = here - steps[slot]
        for qh in range(2):
            if own:
                tile(slot, qh, block)
            else:
                pl.when((block >= 0) & ((block + 1) * 2 * half > table_ref[2 + qh]))(
                    functools.partial(tile, slot, qh, block)
                )
    for qh, ref in enumerate(out_refs):
        rows = slice(qh * half, (qh + 1) * half)
        ref[...] = (accum_ref[rows, :] / total_ref[rows, :]).astype(BF16)


def attend(table, queries, low, pairs, steps, carry=None, close=False):
    rows = low.shape[0]
    half = rows // 2
    width = queries[0].shape[1]
    heads = width // HEAD_DIM
    operands = list(queries) + [low]
    for pair in pairs:
        operands += list(pair)
    operands += list(carry or ())
    scratch = []
    if close:
        out_shape = [shape(half, width)] * 2
        scratch = [pltpu.VMEM((rows, width), F32)] * 3
    else:
        out_shape = [shape(rows, width, F32)] * 3
    fresh = carry is None
    return pl.pallas_call(
        functools.partial(attend_kernel, tuple(steps), heads, fresh, fresh, close),
        in_specs=[scalars()] + [whole()] * len(operands),
        out_specs=[whole()] * len(out_shape),
        out_shape=out_shape,
        scratch_shapes=scratch,
        compiler_params=params(),
        cost_estimate=cost(16 * rows * rows * width * len(pairs), 4 * rows * width),
        name="attend",
    )(table, *operands)


def join_kernel(a_ref, b_ref, out_ref):
    rows = a_ref.shape[0]
    out_ref[:rows, :] = a_ref[...]
    out_ref[rows:, :] = b_ref[...]


def join(a, b):
    return pl.pallas_call(
        join_kernel,
        in_specs=[whole()] * 2,
        out_specs=whole(),
        out_shape=shape(2 * a.shape[0], a.shape[1]),
        compiler_params=params(),
        cost_estimate=cost(0, 8 * a.shape[0] * a.shape[1]),
        name="join",
    )(a, b)


def slice_of(rank):
    return ((rank >> 2) & 1) + 2 * ((rank >> 3) & 1) + 4 * (rank & 1)


def order_kernel(ranks, table_ref, mine_ref, other_ref, out_ref):
    width = mine_ref.shape[1]
    slice_rows = mine_ref.shape[0] // (8 * ranks)
    first_half = table_ref[4] == 0
    mine_at = slice_of(table_ref[0])
    for rank in range(ranks):
        j = mine_at ^ rank
        for k in range(8):
            rows = pl.ds(pl.multiple_of((j * 8 + k) * slice_rows, slice_rows), slice_rows)
            target = slice((k * ranks + rank) * slice_rows, (k * ranks + rank + 1) * slice_rows)
            mine, other = mine_ref[rows, :], other_ref[rows, :]
            out_ref[target, :width] = jnp.where(first_half, mine, other)
            out_ref[target, width:] = jnp.where(first_half, other, mine)


def mix_kernel(plan, fresh, table_ref, w_ref, *refs):
    refs = list(refs)
    out_ref = refs.pop()
    x_refs = [refs.pop(0) for _ in plan]
    place = table_ref[1]
    for part in range(2):
        half, depth = x_refs[0].shape
        rows = slice(part * half, (part + 1) * half)
        total = None if fresh else refs[0][rows, :]
        for (distance, own), x_ref in zip(plan, x_refs):
            if own != part:
                continue
            q = place ^ ((place + distance) % 8)
            k = ((q >> 2) & 1) + 2 * ((q >> 1) & 1) + 4 * (q & 1)
            value = dot(x_ref[...], w_ref[pl.ds(pl.multiple_of(k * depth, depth), depth), :])
            total = value if total is None else total + value
        out_ref[rows, :] = total.astype(out_ref.dtype)


def mix(table, pieces, columns, total=None, dtype=F32):
    half, depth = pieces[0][2].shape
    width = columns.shape[1]
    operands = [columns] + [x for _, _, x in pieces] + ([] if total is None else [total])
    return pl.pallas_call(
        functools.partial(mix_kernel, tuple((d, p) for d, p, _ in pieces), total is None),
        in_specs=[scalars()] + [whole()] * len(operands),
        out_specs=whole(),
        out_shape=shape(2 * half, width, dtype),
        compiler_params=params(),
        cost_estimate=cost(2 * half * depth * width * len(pieces), 2 * half * width),
        name="mix",
    )(table, *operands)


def chips(move):
    pairs = []
    for y in range(SIDE):
        for x in range(SIDE):
            target = move(y, x)
            if target is not None:
                pairs.append((SIDE * y + x, SIDE * target[0] + target[1]))
    return pairs


def per_device(byte_states, patch_spans, doc_lengths, norm_gain, w_query, w_key, w_value, w_out):
    rank = lax.axis_index("seq")
    place = lax.axis_index("tensor")
    seq = lax.axis_size("seq")
    ring = lax.axis_size("tensor")
    byte_rows, depth = byte_states.shape
    rim = byte_rows // 4
    patch_rows = patch_spans.shape[0]
    half = patch_rows // 2
    column = rank % SIDE
    wide = depth // 2
    up = [(i, i + 1) for i in range(seq - 1)]
    down = [(j, i) for i, j in up]

    table = jnp.stack([rank, place]).astype(jnp.int32)

    last, first = byte_states[byte_rows - rim :], byte_states[:rim]
    before = lax.ppermute(last, "seq", up)
    after = lax.ppermute(first, "seq", down)

    slices = 2 * SIDE
    slice_rows = w_out.shape[0] // slices

    def cut(value, bit):
        side = (place // bit) % 2
        wide_half = value.shape[1] // 2
        keep = lax.dynamic_slice_in_dim(value, side * wide_half, wide_half, axis=1)
        give = lax.dynamic_slice_in_dim(value, (1 - side) * wide_half, wide_half, axis=1)
        return keep, give

    def trade(keep, give, bit):
        got = lax.ppermute(give, "tensor", [(i, i ^ bit) for i in range(ring)])
        return jnp.concatenate([keep, got], axis=0)

    columns = lax.dynamic_slice_in_dim(w_out, slice_of(rank) * slice_rows, slice_rows, axis=0)
    for bit in (4, 2):
        columns = trade(*cut(columns, bit), bit)
    keep, give = cut(columns, 1)
    double = lambda value, bit: join(
        value, lax.ppermute(value, "seq", [(i, i ^ bit) for i in range(seq)])
    )

    starts = patch_spans[:, 0:1]
    finish = patch_spans[:, 1:2]
    ends = jnp.cumsum(doc_lengths)
    positions = rank * patch_rows + jnp.arange(patch_rows, dtype=jnp.int32)
    low = jnp.max(jnp.where(ends[None, :] <= positions[:, None], ends[None, :], 0), axis=1)[:, None]
    long_table = jnp.concatenate([table, low[0], low[half], lax.axis_index("dp").astype(jnp.int32)[None]])

    sums, member = pl.pallas_call(
        pool_own_kernel,
        in_specs=[scalars()] + [whole()] * 3,
        out_specs=[whole()] * 2,
        out_shape=[shape(patch_rows, depth, F32), shape(patch_rows, 2 * rim)],
        compiler_params=params(),
        cost_estimate=cost(4 * patch_rows * byte_rows * depth, 2 * byte_rows * depth),
        name="pool_own",
    )(table, byte_states, starts, finish)
    sums, low, long_table, keep, give = lax.optimization_barrier((sums, low, long_table, keep, give))
    columns = trade(keep, give, 1)
    core = lax.axis_index("dp")
    columns = lax.dynamic_slice_in_dim(columns, core * (columns.shape[1] // 2), columns.shape[1] // 2, axis=1)
    pooled = [
        pl.pallas_call(
            functools.partial(pool_rim_kernel, part),
            in_specs=[whole()] * 6,
            out_specs=whole(),
            out_shape=shape(patch_rows, wide),
            compiler_params=params(),
            cost_estimate=cost(4 * patch_rows * rim * wide, 2 * rim * wide),
            name="pool_rim",
        )(before, after, sums, member, starts, finish)
        for part in range(2)
    ]

    right = [(i, (i + 1) % ring) for i in range(ring)]
    left = [(j, i) for i, j in right]
    gain = norm_gain.reshape(2 * ring, 1, wide)
    going = [(x, x) for x in pooled]
    states = [project(table, [(0, part, pooled[part]) for part in range(2)], gain, (w_query, w_key, w_value))]
    weights = states[0][2:]
    states[0] = states[0][:2]
    for distance in range(1, ring // 2):
        if distance > 1:
            early = (states[distance - 2],) if distance == 2 else (states[distance - 2], columns)
            going = [tuple(tie(x, *early) for x in pair) for pair in going]
            columns = double(tie(columns, states[distance - 2]), (4, 8)[distance - 2])
        going = [
            (lax.ppermute(a, "tensor", right), lax.ppermute(b, "tensor", left)) for a, b in going
        ]
        pieces = []
        for part in range(2):
            pieces.append((ring - distance, part, going[part][0]))
            pieces.append((distance, part, going[part][1]))
        if distance < ring // 2 - 1:
            states.append(project(table, pieces, gain, weights, states[-1]))
    last = [
        lax.ppermute(tie(going[0][0], states[-1], columns), "tensor", right),
        lax.ppermute(tie(going[1][1], states[-1], columns), "tensor", left),
    ]
    pieces += [(ring // 2, part, last[part]) for part in range(2)]
    columns = double(tie(columns, states[-1]), 1)
    close = (float(depth * ring), LOG2_E / HEAD_DIM**0.5)
    done = project(table, pieces, gain, weights, states[-1], close)
    queries, pairs = done[0::2], done[1::2]

    lower = chips(lambda y, x: (y + 1, x) if y + 1 < SIDE else None)
    plus = chips(lambda y, x: (y, (x + 1) % SIDE))
    minus = chips(lambda y, x: (y, (x - 1) % SIDE))
    two = chips(lambda y, x: (y, (x + 2) % SIDE))
    slots = {4: [], 1: [], 3: [], 2: []}
    for own in pairs:
        above = lax.ppermute(own, "seq", lower)
        slots[4].append(above)
        slots[1].append(lax.ppermute(jnp.where(column == SIDE - 1, above, own), "seq", plus))
        slots[3].append(lax.ppermute(jnp.where(column == 0, own, above), "seq", minus))
        slots[2].append(lax.ppermute(jnp.where(column < 2, own, above), "seq", two))

    carry = attend(long_table, queries, low, [pairs], [0])
    columns = tie(columns, carry[0])
    others = lax.ppermute(columns, "dp", [(0, 1), (1, 0)])
    columns = pl.pallas_call(
        functools.partial(order_kernel, slices),
        in_specs=[scalars()] + [whole()] * 2,
        out_specs=whole(),
        out_shape=shape(columns.shape[0], 2 * columns.shape[1]),
        compiler_params=params(),
        cost_estimate=cost(0, 8 * columns.shape[0] * columns.shape[1]),
        name="order",
    )(long_table, columns, others)
    for steps in ((4,), (1, 3), (2,)):
        carry = attend(
            long_table, queries, low, [slots[n] for n in steps], steps, carry, steps == (2,)
        )
    attended = carry

    going = [(x, x) for x in attended]
    pieces = [(0, part, attended[part]) for part in range(2)]
    for distance in range(1, ring // 2):
        going = [
            (lax.ppermute(a, "tensor", right), lax.ppermute(b, "tensor", left)) for a, b in going
        ]
        fresh = []
        for part in range(2):
            fresh.append((ring - distance, part, going[part][0]))
            fresh.append((distance, part, going[part][1]))
        if distance < ring // 2 - 1:
            pieces += fresh
    total = mix(long_table, pieces, columns)
    fresh += [
        (ring // 2, 0, lax.ppermute(tie(going[0][0], total), "tensor", right)),
        (ring // 2, 1, lax.ppermute(tie(going[1][1], total), "tensor", left)),
    ]
    return mix(long_table, fresh, columns, total, BF16)


def solution(mesh):
    in_specs = (
        P(("dp", "seq"), "tensor"),
        P(("dp", "seq"), None),
        P("dp"),
        P(),
        P(None, "tensor"),
        P(None, "tensor"),
        P(None, "tensor"),
        P("tensor", None),
    )
    out_specs = P(("dp", "seq"), "tensor")
    return jax.shard_map(
        per_device, mesh=mesh, in_specs=in_specs, out_specs=out_specs, check_vma=False
    )
```

```python
import functools

import jax
import jax.numpy as jnp
from jax import lax
from jax.experimental import pallas as pl
from jax.experimental.pallas import tpu as pltpu
from jax.sharding import PartitionSpec as P

HEAD_DIM = 128
SIDE = 4
VMEM_LIMIT = 16 * 1024 * 1024
FIRST_LIMIT = 44 * 1024 * 1024
NEG = -1e30
LOG2_E = 1.4426950408889634
F32 = jnp.float32
BF16 = jnp.bfloat16


def whole():
    return pl.BlockSpec(memory_space=pltpu.VMEM)


def scalars():
    return pl.BlockSpec(memory_space=pltpu.SMEM)


def params(limit=VMEM_LIMIT):
    return pltpu.CompilerParams(vmem_limit_bytes=limit)


def cost(flops, nbytes):
    return pl.CostEstimate(flops=flops, bytes_accessed=nbytes, transcendentals=0)


def shape(rows, columns, dtype=BF16):
    return jax.ShapeDtypeStruct((rows, columns), dtype)


def dot(a, b):
    return jnp.dot(a, b, preferred_element_type=F32)


def tie(value, *others):
    return lax.optimization_barrier((value, others))[0]


def member_of(first, rows, starts, finish):
    pos = first + lax.broadcasted_iota(jnp.int32, (starts.shape[0], rows), 1)
    return ((pos >= starts) & (pos < finish)).astype(F32).astype(BF16)


def pool_own_kernel(table_ref, bytes_ref, starts_ref, finish_ref, sums_ref, member_ref):
    starts, finish = starts_ref[...], finish_ref[...]
    rows = bytes_ref.shape[0]
    rim = rows // 4
    first = table_ref[0] * rows
    total = None
    for part in range(4):
        member = member_of(first + part * rim, rim, starts, finish)
        value = dot(member, bytes_ref[part * rim : (part + 1) * rim, :])
        total = value if total is None else total + value
    sums_ref[...] = total
    member_ref[:, :rim] = member_of(first - rim, rim, starts, finish)
    member_ref[:, rim:] = member_of(first + rows, rim, starts, finish)


def pool_rim_kernel(part, before_ref, after_ref, sums_ref, member_ref, starts_ref, finish_ref, out_ref):
    rim = before_ref.shape[0]
    width = out_ref.shape[1]
    cols = slice(part * width, (part + 1) * width)
    total = sums_ref[:, cols]
    total += dot(member_ref[:, :rim], before_ref[:, cols])
    total += dot(member_ref[:, rim:], after_ref[:, cols])
    out_ref[...] = (total / (finish_ref[...] - starts_ref[...]).astype(F32)).astype(BF16)


def project_kernel(plan, fresh, close, table_ref, gain_ref, q_ref, k_ref, v_ref, *refs):
    refs = list(refs)
    w_refs = [q_ref, k_ref, v_ref]
    x_refs = [refs.pop(0) for _ in plan]
    if fresh:
        sem = refs.pop()
        kept = refs[2:5]
        copies = [pltpu.make_async_copy(a, b, sem.at[i]) for i, (a, b) in enumerate(zip(w_refs, kept))]
        for copy in copies:
            copy.start()
        w_refs = kept
    else:
        old_sum, old_square = refs.pop(0), refs.pop(0)
    depth = x_refs[0].shape[1]
    columns = q_ref.shape[1]
    blocks = [2 * ((table_ref[1] + distance) % 8) + part for distance, part in plan]
    xs = []
    squares = None
    for ref, block in zip(x_refs, blocks):
        values = ref[...].astype(F32)
        square = values * values
        square = square[:, :128] + square[:, 128:]
        squares = square if squares is None else squares + square
        xs.append((values * gain_ref[block]).astype(BF16))
    if not fresh:
        squares = squares + old_square[...]
    if close:
        features, query_scale = close
        inverse = lax.rsqrt(jnp.sum(squares, axis=1, keepdims=True) / features + 1e-05)
    else:
        refs[1][...] = squares
    half = xs[0].shape[0] // 2
    for i, w_ref in enumerate(w_refs):
        cols = slice(i * columns, (i + 1) * columns)
        if fresh:
            copies[i].wait()
        total = None if fresh else old_sum[:, cols]
        for x, block in zip(xs, blocks):
            value = dot(x, w_ref[pl.ds(pl.multiple_of(block * depth, depth), depth), :])
            total = value if total is None else total + value
        if not close:
            refs[0][:, cols] = total
            continue
        total = total * (inverse * query_scale if i == 0 else inverse)
        for part in range(2):
            rows = slice(part * half, (part + 1) * half)
            if i == 0:
                refs[2 * part][...] = total[rows, :].astype(BF16)
            else:
                refs[2 * part + 1][:, (i - 1) * columns : i * columns] = total[rows, :].astype(BF16)


def project(table, pieces, gain, weights, sums=None, close=None):
    height, depth = pieces[0][2].shape
    columns = weights[0].shape[1]
    plan = tuple((distance, part) for distance, part, _ in pieces)
    rest = [x for _, _, x in pieces] + list(sums or ())
    fresh = sums is None
    scratch = []
    if close:
        out_shape = [shape(height // 2, columns), shape(height // 2, 2 * columns)] * 2
    else:
        out_shape = [shape(height, 3 * columns, F32), shape(height, 128, F32)]
    if fresh:
        out_shape += [shape(*w.shape) for w in weights]
        scratch = [pltpu.SemaphoreType.DMA((3,))]
    w_spec = pl.BlockSpec(memory_space=pltpu.HBM) if fresh else whole()
    return pl.pallas_call(
        functools.partial(project_kernel, plan, fresh, close),
        in_specs=[scalars(), whole()] + [w_spec] * 3 + [whole()] * len(rest),
        out_specs=[whole()] * len(out_shape),
        out_shape=out_shape,
        scratch_shapes=scratch,
        compiler_params=params(FIRST_LIMIT if fresh else VMEM_LIMIT),
        cost_estimate=cost(len(plan) * 6 * height * depth * columns, 6 * depth * columns * len(plan)),
        name="project",
    )(table, gain, *weights, *rest)


def attend_kernel(steps, heads, own, fresh, close, table_ref, *refs):
    refs = list(refs)
    count = len(steps)
    q_refs = [refs.pop(0) for _ in range(2)]
    low_ref = refs.pop(0)
    pair_refs = [(refs.pop(0), refs.pop(0)) for _ in range(count)]
    olds = [] if fresh else [refs.pop(0) for _ in range(3)]
    out_refs = [refs.pop(0) for _ in range(2)] if close else []
    top_ref, total_ref, accum_ref = refs
    half = q_refs[0].shape[0]
    width = heads * HEAD_DIM
    if fresh:
        top_ref[...] = jnp.full(top_ref.shape, NEG, F32)
        total_ref[...] = jnp.zeros(total_ref.shape, F32)
        accum_ref[...] = jnp.zeros(accum_ref.shape, F32)
    else:
        for ref, old in zip((top_ref, total_ref, accum_ref), olds):
            ref[...] = old[...]
    here = table_ref[0]
    ones = jnp.ones((half, HEAD_DIM), BF16)

    def tile(slot, qh, block):
        low = low_ref[qh * half : (qh + 1) * half, :]
        rows = slice(qh * half, (qh + 1) * half)
        parts = (0,) if own and qh == 0 else (0, 1)
        allowed = {}
        for kh in parts:
            key_pos = (2 * block + kh) * half + lax.broadcasted_iota(jnp.int32, (half, half), 1)
            allowed[kh] = key_pos >= low
            if own and kh == qh:
                query_pos = (2 * here + qh) * half + lax.broadcasted_iota(jnp.int32, (half, half), 0)
                allowed[kh] = allowed[kh] & (key_pos <= query_pos)
        for head in range(heads):
            cols = slice(head * HEAD_DIM, (head + 1) * HEAD_DIM)
            value_cols = slice(width + head * HEAD_DIM, width + (head + 1) * HEAD_DIM)
            query = q_refs[qh][:, cols]
            scores = {}
            for kh in parts:
                value = lax.dot_general(
                    query,
                    pair_refs[slot][kh][:, cols],
                    (((1,), (1,)), ((), ())),
                    preferred_element_type=F32,
                )
                scores[kh] = jnp.where(allowed[kh], value, NEG)
            best = scores[0] if len(parts) == 1 else jnp.maximum(scores[0], scores[1])
            top = top_ref[rows, cols]
            new_top = jnp.maximum(top, jnp.max(best, axis=1, keepdims=True))
            fade = jnp.exp2(top - new_top)
            update = None
            for kh in parts:
                weights = jnp.exp2(scores[kh] - new_top[:, 0:1]).astype(BF16)
                values = jnp.concatenate([pair_refs[slot][kh][:, value_cols], ones], axis=1)
                value = dot(weights, values)
                update = value if update is None else update + value
            accum_ref[rows, cols] = accum_ref[rows, cols] * fade + update[:, :HEAD_DIM]
            total_ref[rows, cols] = total_ref[rows, cols] * fade + update[:, HEAD_DIM:]
            top_ref[rows, cols] = new_top

    for slot in range(count):
        block = here - steps[slot]
        for qh in range(2):
            if own:
                tile(slot, qh, block)
            else:
                pl.when((block >= 0) & ((block + 1) * 2 * half > table_ref[2 + qh]))(
                    functools.partial(tile, slot, qh, block)
                )
    for qh, ref in enumerate(out_refs):
        rows = slice(qh * half, (qh + 1) * half)
        ref[...] = (accum_ref[rows, :] / total_ref[rows, :]).astype(BF16)


def attend(table, queries, low, pairs, steps, carry=None, close=False):
    rows = low.shape[0]
    half = rows // 2
    width = queries[0].shape[1]
    heads = width // HEAD_DIM
    operands = list(queries) + [low]
    for pair in pairs:
        operands += list(pair)
    operands += list(carry or ())
    scratch = []
    if close:
        out_shape = [shape(half, width)] * 2
        scratch = [pltpu.VMEM((rows, width), F32)] * 3
    else:
        out_shape = [shape(rows, width, F32)] * 3
    fresh = carry is None
    return pl.pallas_call(
        functools.partial(attend_kernel, tuple(steps), heads, fresh, fresh, close),
        in_specs=[scalars()] + [whole()] * len(operands),
        out_specs=[whole()] * len(out_shape),
        out_shape=out_shape,
        scratch_shapes=scratch,
        compiler_params=params(),
        cost_estimate=cost(16 * rows * rows * width * len(pairs), 4 * rows * width),
        name="attend",
    )(table, *operands)


def join_kernel(a_ref, b_ref, out_ref):
    rows = a_ref.shape[0]
    out_ref[:rows, :] = a_ref[...]
    out_ref[rows:, :] = b_ref[...]


def join(a, b):
    return pl.pallas_call(
        join_kernel,
        in_specs=[whole()] * 2,
        out_specs=whole(),
        out_shape=shape(2 * a.shape[0], a.shape[1]),
        compiler_params=params(),
        cost_estimate=cost(0, 8 * a.shape[0] * a.shape[1]),
        name="join",
    )(a, b)


def slice_of(rank):
    return ((rank >> 2) & 1) + 2 * ((rank >> 3) & 1) + 4 * (rank & 1)


def order_kernel(ranks, table_ref, mine_ref, other_ref, out_ref):
    width = mine_ref.shape[1]
    slice_rows = mine_ref.shape[0] // (8 * ranks)
    first_half = table_ref[4] == 0
    mine_at = slice_of(table_ref[0])
    for rank in range(ranks):
        j = mine_at ^ rank
        for k in range(8):
            rows = pl.ds(pl.multiple_of((j * 8 + k) * slice_rows, slice_rows), slice_rows)
            target = slice((k * ranks + rank) * slice_rows, (k * ranks + rank + 1) * slice_rows)
            mine, other = mine_ref[rows, :], other_ref[rows, :]
            out_ref[target, :width] = jnp.where(first_half, mine, other)
            out_ref[target, width:] = jnp.where(first_half, other, mine)


def mix_kernel(plan, fresh, table_ref, w_ref, *refs):
    refs = list(refs)
    out_ref = refs.pop()
    x_refs = [refs.pop(0) for _ in plan]
    place = table_ref[1]
    for part in range(2):
        half, depth = x_refs[0].shape
        rows = slice(part * half, (part + 1) * half)
        total = None if fresh else refs[0][rows, :]
        for (distance, own), x_ref in zip(plan, x_refs):
            if own != part:
                continue
            q = place ^ ((place + distance) % 8)
            k = ((q >> 2) & 1) + 2 * ((q >> 1) & 1) + 4 * (q & 1)
            value = dot(x_ref[...], w_ref[pl.ds(pl.multiple_of(k * depth, depth), depth), :])
            total = value if total is None else total + value
        out_ref[rows, :] = total.astype(out_ref.dtype)


def mix(table, pieces, columns, total=None, dtype=F32):
    half, depth = pieces[0][2].shape
    width = columns.shape[1]
    operands = [columns] + [x for _, _, x in pieces] + ([] if total is None else [total])
    return pl.pallas_call(
        functools.partial(mix_kernel, tuple((d, p) for d, p, _ in pieces), total is None),
        in_specs=[scalars()] + [whole()] * len(operands),
        out_specs=whole(),
        out_shape=shape(2 * half, width, dtype),
        compiler_params=params(),
        cost_estimate=cost(2 * half * depth * width * len(pieces), 2 * half * width),
        name="mix",
    )(table, *operands)


def chips(move):
    pairs = []
    for y in range(SIDE):
        for x in range(SIDE):
            target = move(y, x)
            if target is not None:
                pairs.append((SIDE * y + x, SIDE * target[0] + target[1]))
    return pairs


def per_device(byte_states, patch_spans, doc_lengths, norm_gain, w_query, w_key, w_value, w_out):
    rank = lax.axis_index("seq")
    place = lax.axis_index("tensor")
    seq = lax.axis_size("seq")
    ring = lax.axis_size("tensor")
    byte_rows, depth = byte_states.shape
    rim = byte_rows // 4
    patch_rows = patch_spans.shape[0]
    half = patch_rows // 2
    column = rank % SIDE
    wide = depth // 2
    up = [(i, i + 1) for i in range(seq - 1)]
    down = [(j, i) for i, j in up]

    table = jnp.stack([rank, place]).astype(jnp.int32)

    last, first = byte_states[byte_rows - rim :], byte_states[:rim]
    before = lax.ppermute(last, "seq", up)
    after = lax.ppermute(first, "seq", down)

    slices = 2 * SIDE
    slice_rows = w_out.shape[0] // slices

    def cut(value, bit):
        side = (place // bit) % 2
        wide_half = value.shape[1] // 2
        keep = lax.dynamic_slice_in_dim(value, side * wide_half, wide_half, axis=1)
        give = lax.dynamic_slice_in_dim(value, (1 - side) * wide_half, wide_half, axis=1)
        return keep, give

    def trade(keep, give, bit):
        got = lax.ppermute(give, "tensor", [(i, i ^ bit) for i in range(ring)])
        return jnp.concatenate([keep, got], axis=0)

    columns = lax.dynamic_slice_in_dim(w_out, slice_of(rank) * slice_rows, slice_rows, axis=0)
    for bit in (4, 2):
        columns = trade(*cut(columns, bit), bit)
    keep, give = cut(columns, 1)
    double = lambda value, bit: join(
        value, lax.ppermute(value, "seq", [(i, i ^ bit) for i in range(seq)])
    )

    starts = patch_spans[:, 0:1]
    finish = patch_spans[:, 1:2]
    ends = jnp.cumsum(doc_lengths)
    positions = rank * patch_rows + jnp.arange(patch_rows, dtype=jnp.int32)
    low = jnp.max(jnp.where(ends[None, :] <= positions[:, None], ends[None, :], 0), axis=1)[:, None]
    long_table = jnp.concatenate([table, low[0], low[half], lax.axis_index("dp").astype(jnp.int32)[None]])

    sums, member = pl.pallas_call(
        pool_own_kernel,
        in_specs=[scalars()] + [whole()] * 3,
        out_specs=[whole()] * 2,
        out_shape=[shape(patch_rows, depth, F32), shape(patch_rows, 2 * rim)],
        compiler_params=params(),
        cost_estimate=cost(4 * patch_rows * byte_rows * depth, 2 * byte_rows * depth),
        name="pool_own",
    )(table, byte_states, starts, finish)
    sums, low, long_table, keep, give = lax.optimization_barrier((sums, low, long_table, keep, give))
    columns = trade(keep, give, 1)
    core = lax.axis_index("dp")
    columns = lax.dynamic_slice_in_dim(columns, core * (columns.shape[1] // 2), columns.shape[1] // 2, axis=1)
    pooled = [
        pl.pallas_call(
            functools.partial(pool_rim_kernel, part),
            in_specs=[whole()] * 6,
            out_specs=whole(),
            out_shape=shape(patch_rows, wide),
            compiler_params=params(),
            cost_estimate=cost(4 * patch_rows * rim * wide, 2 * rim * wide),
            name="pool_rim",
        )(before, after, sums, member, starts, finish)
        for part in range(2)
    ]

    right = [(i, (i + 1) % ring) for i in range(ring)]
    left = [(j, i) for i, j in right]
    gain = norm_gain.reshape(2 * ring, 1, wide)
    going = [(x, x) for x in pooled]
    weights = (w_query, w_key, w_value)
    pieces = [(0, part, pooled[part]) for part in range(2)]
    states = []
    for distance in range(1, ring // 2):
        early = () if distance < 3 else (states[distance - 3], columns)
        if early:
            going = [tuple(tie(x, *early) for x in pair) for pair in going]
        if distance > 1:
            columns = double(tie(columns, states[distance - 3]) if early else columns, (4, 8)[distance - 2])
        going = [
            (lax.ppermute(a, "tensor", right), lax.ppermute(b, "tensor", left)) for a, b in going
        ]
        for part in range(2):
            pieces.append((ring - distance, part, going[part][0]))
            pieces.append((distance, part, going[part][1]))
        if distance == 1:
            first = project(table, pieces, gain, weights)
            states.append(first[:2])
            weights = first[2:]
        elif distance < ring // 2 - 1:
            states.append(project(table, pieces, gain, weights, states[-1]))
        if distance < ring // 2 - 1:
            pieces = []
    last = [
        lax.ppermute(tie(going[0][0], states[-1], columns), "tensor", right),
        lax.ppermute(tie(going[1][1], states[-1], columns), "tensor", left),
    ]
    pieces += [(ring // 2, part, last[part]) for part in range(2)]
    columns = double(tie(columns, states[-1]), 1)
    close = (float(depth * ring), LOG2_E / HEAD_DIM**0.5)
    done = project(table, pieces, gain, weights, states[-1], close)
    queries, pairs = done[0::2], done[1::2]

    lower = chips(lambda y, x: (y + 1, x) if y + 1 < SIDE else None)
    plus = chips(lambda y, x: (y, (x + 1) % SIDE))
    minus = chips(lambda y, x: (y, (x - 1) % SIDE))
    two = chips(lambda y, x: (y, (x + 2) % SIDE))
    slots = {4: [], 1: [], 3: [], 2: []}
    for own in pairs:
        above = lax.ppermute(own, "seq", lower)
        slots[4].append(above)
        slots[1].append(lax.ppermute(jnp.where(column == SIDE - 1, above, own), "seq", plus))
        slots[3].append(lax.ppermute(jnp.where(column == 0, own, above), "seq", minus))
        slots[2].append(lax.ppermute(jnp.where(column < 2, own, above), "seq", two))

    carry = attend(long_table, queries, low, [pairs], [0])
    columns = tie(columns, carry[0])
    others = lax.ppermute(columns, "dp", [(0, 1), (1, 0)])
    columns = pl.pallas_call(
        functools.partial(order_kernel, slices),
        in_specs=[scalars()] + [whole()] * 2,
        out_specs=whole(),
        out_shape=shape(columns.shape[0], 2 * columns.shape[1]),
        compiler_params=params(),
        cost_estimate=cost(0, 8 * columns.shape[0] * columns.shape[1]),
        name="order",
    )(long_table, columns, others)
    for steps in ((4,), (1, 3), (2,)):
        carry = attend(
            long_table, queries, low, [slots[n] for n in steps], steps, carry, steps == (2,)
        )
    attended = carry

    going = [(x, x) for x in attended]
    pieces = [(0, part, attended[part]) for part in range(2)]
    for distance in range(1, ring // 2):
        going = [
            (lax.ppermute(a, "tensor", right), lax.ppermute(b, "tensor", left)) for a, b in going
        ]
        fresh = []
        for part in range(2):
            fresh.append((ring - distance, part, going[part][0]))
            fresh.append((distance, part, going[part][1]))
        if distance < ring // 2 - 1:
            pieces += fresh
    total = mix(long_table, pieces, columns)
    fresh += [
        (ring // 2, 0, lax.ppermute(tie(going[0][0], total), "tensor", right)),
        (ring // 2, 1, lax.ppermute(tie(going[1][1], total), "tensor", left)),
    ]
    return mix(long_table, fresh, columns, total, BF16)


def solution(mesh):
    in_specs = (
        P(("dp", "seq"), "tensor"),
        P(("dp", "seq"), None),
        P("dp"),
        P(),
        P(None, "tensor"),
        P(None, "tensor"),
        P(None, "tensor"),
        P("tensor", None),
    )
    out_specs = P(("dp", "seq"), "tensor")
    return jax.shard_map(
        per_device, mesh=mesh, in_specs=in_specs, out_specs=out_specs, check_vma=False
    )
```

```python
import functools

import jax
import jax.numpy as jnp
from jax import lax
from jax.experimental import pallas as pl
from jax.experimental.pallas import tpu as pltpu
from jax.sharding import PartitionSpec as P

HEAD_DIM = 128
SIDE = 4
VMEM_LIMIT = 16 * 1024 * 1024
FIRST_LIMIT = 44 * 1024 * 1024
NEG = -1e30
LOG2_E = 1.4426950408889634
F32 = jnp.float32
BF16 = jnp.bfloat16


def whole():
    return pl.BlockSpec(memory_space=pltpu.VMEM)


def scalars():
    return pl.BlockSpec(memory_space=pltpu.SMEM)


def params(limit=VMEM_LIMIT):
    return pltpu.CompilerParams(vmem_limit_bytes=limit)


def cost(flops, nbytes):
    return pl.CostEstimate(flops=flops, bytes_accessed=nbytes, transcendentals=0)


def shape(rows, columns, dtype=BF16):
    return jax.ShapeDtypeStruct((rows, columns), dtype)


def dot(a, b):
    return jnp.dot(a, b, preferred_element_type=F32)


def tie(value, *others):
    return lax.optimization_barrier((value, others))[0]


def member_of(first, rows, starts, finish):
    pos = first + lax.broadcasted_iota(jnp.int32, (starts.shape[0], rows), 1)
    return ((pos >= starts) & (pos < finish)).astype(F32).astype(BF16)


def pool_own_kernel(table_ref, bytes_ref, starts_ref, finish_ref, sums_ref, member_ref):
    starts, finish = starts_ref[...], finish_ref[...]
    rows = bytes_ref.shape[0]
    rim = rows // 4
    first = table_ref[0] * rows
    total = None
    for part in range(4):
        member = member_of(first + part * rim, rim, starts, finish)
        value = dot(member, bytes_ref[part * rim : (part + 1) * rim, :])
        total = value if total is None else total + value
    sums_ref[...] = total
    member_ref[:, :rim] = member_of(first - rim, rim, starts, finish)
    member_ref[:, rim:] = member_of(first + rows, rim, starts, finish)


def pool_rim_kernel(part, before_ref, after_ref, sums_ref, member_ref, starts_ref, finish_ref, out_ref):
    rim = before_ref.shape[0]
    width = out_ref.shape[1]
    cols = slice(part * width, (part + 1) * width)
    total = sums_ref[:, cols]
    total += dot(member_ref[:, :rim], before_ref[:, cols])
    total += dot(member_ref[:, rim:], after_ref[:, cols])
    out_ref[...] = (total / (finish_ref[...] - starts_ref[...]).astype(F32)).astype(BF16)


def project_kernel(plan, fresh, close, table_ref, gain_ref, q_ref, k_ref, v_ref, *refs):
    refs = list(refs)
    w_refs = [q_ref, k_ref, v_ref]
    x_refs = [refs.pop(0) for _ in plan]
    if fresh:
        sem = refs.pop()
        kept = refs[2:5]
        copies = [pltpu.make_async_copy(a, b, sem.at[i]) for i, (a, b) in enumerate(zip(w_refs, kept))]
        for copy in copies:
            copy.start()
        w_refs = kept
    else:
        old_sum, old_square = refs.pop(0), refs.pop(0)
    depth = x_refs[0].shape[1]
    columns = q_ref.shape[1]
    blocks = [2 * ((table_ref[1] + distance) % 8) + part for distance, part in plan]
    xs = []
    squares = None
    for ref, block in zip(x_refs, blocks):
        values = ref[...].astype(F32)
        square = values * values
        square = square[:, :128] + square[:, 128:]
        squares = square if squares is None else squares + square
        xs.append((values * gain_ref[block]).astype(BF16))
    if not fresh:
        squares = squares + old_square[...]
    if close:
        features, query_scale = close
        inverse = lax.rsqrt(jnp.sum(squares, axis=1, keepdims=True) / features + 1e-05)
    else:
        refs[1][...] = squares
    half = xs[0].shape[0] // 2
    for i, w_ref in enumerate(w_refs):
        cols = slice(i * columns, (i + 1) * columns)
        if fresh:
            copies[i].wait()
        total = None if fresh else old_sum[:, cols]
        for x, block in zip(xs, blocks):
            value = dot(x, w_ref[pl.ds(pl.multiple_of(block * depth, depth), depth), :])
            total = value if total is None else total + value
        if not close:
            refs[0][:, cols] = total
            continue
        total = total * (inverse * query_scale if i == 0 else inverse)
        for part in range(2):
            rows = slice(part * half, (part + 1) * half)
            if i == 0:
                refs[2 * part][...] = total[rows, :].astype(BF16)
            else:
                refs[2 * part + 1][:, (i - 1) * columns : i * columns] = total[rows, :].astype(BF16)


def project(table, pieces, gain, weights, sums=None, close=None):
    height, depth = pieces[0][2].shape
    columns = weights[0].shape[1]
    plan = tuple((distance, part) for distance, part, _ in pieces)
    rest = [x for _, _, x in pieces] + list(sums or ())
    fresh = sums is None
    scratch = []
    if close:
        out_shape = [shape(height // 2, columns), shape(height // 2, 2 * columns)] * 2
    else:
        out_shape = [shape(height, 3 * columns, F32), shape(height, 128, F32)]
    if fresh:
        out_shape += [shape(*w.shape) for w in weights]
        scratch = [pltpu.SemaphoreType.DMA((3,))]
    w_spec = pl.BlockSpec(memory_space=pltpu.HBM) if fresh else whole()
    return pl.pallas_call(
        functools.partial(project_kernel, plan, fresh, close),
        in_specs=[scalars(), whole()] + [w_spec] * 3 + [whole()] * len(rest),
        out_specs=[whole()] * len(out_shape),
        out_shape=out_shape,
        scratch_shapes=scratch,
        compiler_params=params(FIRST_LIMIT if fresh else VMEM_LIMIT),
        cost_estimate=cost(len(plan) * 6 * height * depth * columns, 6 * depth * columns * len(plan)),
        name="project",
    )(table, gain, *weights, *rest)


def attend_kernel(steps, heads, own, fresh, close, table_ref, *refs):
    refs = list(refs)
    count = len(steps)
    q_refs = [refs.pop(0) for _ in range(2)]
    low_ref = refs.pop(0)
    pair_refs = [(refs.pop(0), refs.pop(0)) for _ in range(count)]
    olds = [] if fresh else [refs.pop(0) for _ in range(3)]
    out_refs = [refs.pop(0) for _ in range(2)] if close else []
    top_ref, total_ref, accum_ref = refs
    half = q_refs[0].shape[0]
    width = heads * HEAD_DIM
    if fresh:
        top_ref[...] = jnp.full(top_ref.shape, NEG, F32)
        total_ref[...] = jnp.zeros(total_ref.shape, F32)
        accum_ref[...] = jnp.zeros(accum_ref.shape, F32)
    else:
        for ref, old in zip((top_ref, total_ref, accum_ref), olds):
            ref[...] = old[...]
    here = table_ref[0]
    ones = jnp.ones((half, HEAD_DIM), BF16)

    def tile(slot, qh, block):
        low = low_ref[qh * half : (qh + 1) * half, :]
        rows = slice(qh * half, (qh + 1) * half)
        parts = (0,) if own and qh == 0 else (0, 1)
        allowed = {}
        for kh in parts:
            key_pos = (2 * block + kh) * half + lax.broadcasted_iota(jnp.int32, (half, half), 1)
            allowed[kh] = key_pos >= low
            if own and kh == qh:
                query_pos = (2 * here + qh) * half + lax.broadcasted_iota(jnp.int32, (half, half), 0)
                allowed[kh] = allowed[kh] & (key_pos <= query_pos)
        for head in range(heads):
            cols = slice(head * HEAD_DIM, (head + 1) * HEAD_DIM)
            value_cols = slice(width + head * HEAD_DIM, width + (head + 1) * HEAD_DIM)
            query = q_refs[qh][:, cols]
            scores = {}
            for kh in parts:
                value = lax.dot_general(
                    query,
                    pair_refs[slot][kh][:, cols],
                    (((1,), (1,)), ((), ())),
                    preferred_element_type=F32,
                )
                scores[kh] = jnp.where(allowed[kh], value, NEG)
            best = scores[0] if len(parts) == 1 else jnp.maximum(scores[0], scores[1])
            top = top_ref[rows, cols]
            new_top = jnp.maximum(top, jnp.max(best, axis=1, keepdims=True))
            fade = jnp.exp2(top - new_top)
            update = None
            for kh in parts:
                weights = jnp.exp2(scores[kh] - new_top[:, 0:1]).astype(BF16)
                values = jnp.concatenate([pair_refs[slot][kh][:, value_cols], ones], axis=1)
                value = dot(weights, values)
                update = value if update is None else update + value
            accum_ref[rows, cols] = accum_ref[rows, cols] * fade + update[:, :HEAD_DIM]
            total_ref[rows, cols] = total_ref[rows, cols] * fade + update[:, HEAD_DIM:]
            top_ref[rows, cols] = new_top

    for slot in range(count):
        block = here - steps[slot]
        for qh in range(2):
            if own:
                tile(slot, qh, block)
            else:
                pl.when((block >= 0) & ((block + 1) * 2 * half > table_ref[2 + qh]))(
                    functools.partial(tile, slot, qh, block)
                )
    for qh, ref in enumerate(out_refs):
        rows = slice(qh * half, (qh + 1) * half)
        ref[...] = (accum_ref[rows, :] / total_ref[rows, :]).astype(BF16)


def attend(table, queries, low, pairs, steps, carry=None, close=False):
    rows = low.shape[0]
    half = rows // 2
    width = queries[0].shape[1]
    heads = width // HEAD_DIM
    operands = list(queries) + [low]
    for pair in pairs:
        operands += list(pair)
    operands += list(carry or ())
    scratch = []
    if close:
        out_shape = [shape(half, width)] * 2
        scratch = [pltpu.VMEM((rows, width), F32)] * 3
    else:
        out_shape = [shape(rows, width, F32)] * 3
    fresh = carry is None
    return pl.pallas_call(
        functools.partial(attend_kernel, tuple(steps), heads, fresh, fresh, close),
        in_specs=[scalars()] + [whole()] * len(operands),
        out_specs=[whole()] * len(out_shape),
        out_shape=out_shape,
        scratch_shapes=scratch,
        compiler_params=params(),
        cost_estimate=cost(16 * rows * rows * width * len(pairs), 4 * rows * width),
        name="attend",
    )(table, *operands)


def join_kernel(a_ref, b_ref, out_ref):
    rows = a_ref.shape[0]
    out_ref[:rows, :] = a_ref[...]
    out_ref[rows:, :] = b_ref[...]


def join(a, b):
    return pl.pallas_call(
        join_kernel,
        in_specs=[whole()] * 2,
        out_specs=whole(),
        out_shape=shape(2 * a.shape[0], a.shape[1]),
        compiler_params=params(),
        cost_estimate=cost(0, 8 * a.shape[0] * a.shape[1]),
        name="join",
    )(a, b)


def slice_of(rank):
    return (rank & 1) + 2 * ((rank >> 2) & 1) + 4 * ((rank >> 3) & 1)


def order_kernel(ranks, table_ref, mine_ref, other_ref, out_ref):
    width = mine_ref.shape[1]
    slice_rows = mine_ref.shape[0] // (8 * ranks)
    first_half = table_ref[4] == 0
    mine_at = slice_of(table_ref[0])
    for rank in range(ranks):
        j = mine_at ^ rank
        for k in range(8):
            rows = pl.ds(pl.multiple_of((j * 8 + k) * slice_rows, slice_rows), slice_rows)
            target = slice((k * ranks + rank) * slice_rows, (k * ranks + rank + 1) * slice_rows)
            mine, other = mine_ref[rows, :], other_ref[rows, :]
            out_ref[target, :width] = jnp.where(first_half, mine, other)
            out_ref[target, width:] = jnp.where(first_half, other, mine)


def mix_kernel(plan, fresh, table_ref, w_ref, *refs):
    refs = list(refs)
    out_ref = refs.pop()
    x_refs = [refs.pop(0) for _ in plan]
    place = table_ref[1]
    for part in range(2):
        half, depth = x_refs[0].shape
        rows = slice(part * half, (part + 1) * half)
        total = None if fresh else refs[0][rows, :]
        for (distance, own), x_ref in zip(plan, x_refs):
            if own != part:
                continue
            q = place ^ ((place + distance) % 8)
            k = ((q >> 2) & 1) + 2 * ((q >> 1) & 1) + 4 * (q & 1)
            value = dot(x_ref[...], w_ref[pl.ds(pl.multiple_of(k * depth, depth), depth), :])
            total = value if total is None else total + value
        out_ref[rows, :] = total.astype(out_ref.dtype)


def mix(table, pieces, columns, total=None, dtype=F32):
    half, depth = pieces[0][2].shape
    width = columns.shape[1]
    operands = [columns] + [x for _, _, x in pieces] + ([] if total is None else [total])
    return pl.pallas_call(
        functools.partial(mix_kernel, tuple((d, p) for d, p, _ in pieces), total is None),
        in_specs=[scalars()] + [whole()] * len(operands),
        out_specs=whole(),
        out_shape=shape(2 * half, width, dtype),
        compiler_params=params(),
        cost_estimate=cost(2 * half * depth * width * len(pieces), 2 * half * width),
        name="mix",
    )(table, *operands)


def chips(move):
    pairs = []
    for y in range(SIDE):
        for x in range(SIDE):
            target = move(y, x)
            if target is not None:
                pairs.append((SIDE * y + x, SIDE * target[0] + target[1]))
    return pairs


def per_device(byte_states, patch_spans, doc_lengths, norm_gain, w_query, w_key, w_value, w_out):
    rank = lax.axis_index("seq")
    place = lax.axis_index("tensor")
    seq = lax.axis_size("seq")
    ring = lax.axis_size("tensor")
    byte_rows, depth = byte_states.shape
    rim = byte_rows // 4
    patch_rows = patch_spans.shape[0]
    half = patch_rows // 2
    column = rank % SIDE
    wide = depth // 2
    up = [(i, i + 1) for i in range(seq - 1)]
    down = [(j, i) for i, j in up]

    table = jnp.stack([rank, place]).astype(jnp.int32)

    last, first = byte_states[byte_rows - rim :], byte_states[:rim]
    before = lax.ppermute(last, "seq", up)
    after = lax.ppermute(first, "seq", down)

    slices = 2 * SIDE
    slice_rows = w_out.shape[0] // slices

    def cut(value, bit):
        side = (place // bit) % 2
        wide_half = value.shape[1] // 2
        keep = lax.dynamic_slice_in_dim(value, side * wide_half, wide_half, axis=1)
        give = lax.dynamic_slice_in_dim(value, (1 - side) * wide_half, wide_half, axis=1)
        return keep, give

    def trade(keep, give, bit):
        got = lax.ppermute(give, "tensor", [(i, i ^ bit) for i in range(ring)])
        return jnp.concatenate([keep, got], axis=0)

    columns = lax.dynamic_slice_in_dim(w_out, slice_of(rank) * slice_rows, slice_rows, axis=0)
    for bit in (4, 2):
        columns = trade(*cut(columns, bit), bit)
    keep, give = cut(columns, 1)
    double = lambda value, bit: join(
        value, lax.ppermute(value, "seq", [(i, i ^ bit) for i in range(seq)])
    )

    starts = patch_spans[:, 0:1]
    finish = patch_spans[:, 1:2]
    ends = jnp.cumsum(doc_lengths)
    positions = rank * patch_rows + jnp.arange(patch_rows, dtype=jnp.int32)
    low = jnp.max(jnp.where(ends[None, :] <= positions[:, None], ends[None, :], 0), axis=1)[:, None]
    long_table = jnp.concatenate([table, low[0], low[half], lax.axis_index("dp").astype(jnp.int32)[None]])

    sums, member = pl.pallas_call(
        pool_own_kernel,
        in_specs=[scalars()] + [whole()] * 3,
        out_specs=[whole()] * 2,
        out_shape=[shape(patch_rows, depth, F32), shape(patch_rows, 2 * rim)],
        compiler_params=params(),
        cost_estimate=cost(4 * patch_rows * byte_rows * depth, 2 * byte_rows * depth),
        name="pool_own",
    )(table, byte_states, starts, finish)
    sums, low, long_table, keep, give = lax.optimization_barrier((sums, low, long_table, keep, give))
    columns = trade(keep, give, 1)
    core = lax.axis_index("dp")
    columns = lax.dynamic_slice_in_dim(columns, core * (columns.shape[1] // 2), columns.shape[1] // 2, axis=1)
    pooled = [
        pl.pallas_call(
            functools.partial(pool_rim_kernel, part),
            in_specs=[whole()] * 6,
            out_specs=whole(),
            out_shape=shape(patch_rows, wide),
            compiler_params=params(),
            cost_estimate=cost(4 * patch_rows * rim * wide, 2 * rim * wide),
            name="pool_rim",
        )(before, after, sums, member, starts, finish)
        for part in range(2)
    ]

    right = [(i, (i + 1) % ring) for i in range(ring)]
    left = [(j, i) for i, j in right]
    gain = norm_gain.reshape(2 * ring, 1, wide)
    going = [(x, x) for x in pooled]
    weights = (w_query, w_key, w_value)
    pieces = [(0, part, pooled[part]) for part in range(2)]
    states = []
    for distance in range(1, ring // 2):
        early = () if distance < 3 else (states[distance - 3],)
        if early:
            going = [tuple(tie(x, *early) for x in pair) for pair in going]
            columns = double(tie(columns, *early), 1)
        going = [
            (lax.ppermute(a, "tensor", right), lax.ppermute(b, "tensor", left)) for a, b in going
        ]
        for part in range(2):
            pieces.append((ring - distance, part, going[part][0]))
            pieces.append((distance, part, going[part][1]))
        if distance == 1:
            first = project(table, pieces, gain, weights)
            states.append(first[:2])
            weights = first[2:]
        elif distance < ring // 2 - 1:
            states.append(project(table, pieces, gain, weights, states[-1]))
        if distance < ring // 2 - 1:
            pieces = []
    last = [
        lax.ppermute(tie(going[0][0], states[-1], columns), "tensor", right),
        lax.ppermute(tie(going[1][1], states[-1], columns), "tensor", left),
    ]
    pieces += [(ring // 2, part, last[part]) for part in range(2)]
    close = (float(depth * ring), LOG2_E / HEAD_DIM**0.5)
    done = project(table, pieces, gain, weights, states[-1], close)
    queries, pairs = done[0::2], done[1::2]

    lower = chips(lambda y, x: (y + 1, x) if y + 1 < SIDE else None)
    plus = chips(lambda y, x: (y, (x + 1) % SIDE))
    minus = chips(lambda y, x: (y, (x - 1) % SIDE))
    two = chips(lambda y, x: (y, (x + 2) % SIDE))
    slots = {4: [], 1: [], 3: [], 2: []}
    for own in pairs:
        above = lax.ppermute(own, "seq", lower)
        slots[4].append(above)
        slots[1].append(lax.ppermute(jnp.where(column == SIDE - 1, above, own), "seq", plus))
        slots[3].append(lax.ppermute(jnp.where(column == 0, own, above), "seq", minus))
        slots[2].append(lax.ppermute(jnp.where(column < 2, own, above), "seq", two))

    carry = attend(long_table, queries, low, [pairs], [0])
    columns = double(tie(columns, carry[0]), 4)
    columns = double(tie(columns, slots[3][0]), 8)
    for steps in ((4,), (1, 3), (2,)):
        carry = attend(
            long_table, queries, low, [slots[n] for n in steps], steps, carry, steps == (2,)
        )
    attended = carry

    going = [(x, x) for x in attended]
    pieces = [(0, part, attended[part]) for part in range(2)]
    for distance in range(1, ring // 2):
        going = [
            (lax.ppermute(a, "tensor", right), lax.ppermute(b, "tensor", left)) for a, b in going
        ]
        if distance == 1:
            columns = tie(columns, attended[1])
            others = lax.ppermute(columns, "dp", [(0, 1), (1, 0)])
        fresh = []
        for part in range(2):
            fresh.append((ring - distance, part, going[part][0]))
            fresh.append((distance, part, going[part][1]))
        if distance < ring // 2 - 1:
            pieces += fresh
    columns = pl.pallas_call(
        functools.partial(order_kernel, slices),
        in_specs=[scalars()] + [whole()] * 2,
        out_specs=whole(),
        out_shape=shape(columns.shape[0], 2 * columns.shape[1]),
        compiler_params=params(),
        cost_estimate=cost(0, 8 * columns.shape[0] * columns.shape[1]),
        name="order",
    )(long_table, columns, others)
    total = mix(long_table, pieces, columns)
    fresh += [
        (ring // 2, 0, lax.ppermute(tie(going[0][0], total), "tensor", right)),
        (ring // 2, 1, lax.ppermute(tie(going[1][1], total), "tensor", left)),
    ]
    return mix(long_table, fresh, columns, total, BF16)


def solution(mesh):
    in_specs = (
        P(("dp", "seq"), "tensor"),
        P(("dp", "seq"), None),
        P("dp"),
        P(),
        P(None, "tensor"),
        P(None, "tensor"),
        P(None, "tensor"),
        P("tensor", None),
    )
    out_specs = P(("dp", "seq"), "tensor")
    return jax.shard_map(
        per_device, mesh=mesh, in_specs=in_specs, out_specs=out_specs, check_vma=False
    )
```

```python
import functools

import jax
import jax.numpy as jnp
from jax import lax
from jax.experimental import pallas as pl
from jax.experimental.pallas import tpu as pltpu
from jax.sharding import PartitionSpec as P

HEAD_DIM = 128
SIDE = 4
VMEM_LIMIT = 16 * 1024 * 1024
FIRST_LIMIT = 44 * 1024 * 1024
NEG = -1e30
LOG2_E = 1.4426950408889634
F32 = jnp.float32
BF16 = jnp.bfloat16


def whole():
    return pl.BlockSpec(memory_space=pltpu.VMEM)


def scalars():
    return pl.BlockSpec(memory_space=pltpu.SMEM)


def params(limit=VMEM_LIMIT):
    return pltpu.CompilerParams(vmem_limit_bytes=limit)


def cost(flops, nbytes):
    return pl.CostEstimate(flops=flops, bytes_accessed=nbytes, transcendentals=0)


def shape(rows, columns, dtype=BF16):
    return jax.ShapeDtypeStruct((rows, columns), dtype)


def dot(a, b):
    return jnp.dot(a, b, preferred_element_type=F32)


def tie(value, *others):
    return lax.optimization_barrier((value, others))[0]


def member_of(first, rows, starts, finish):
    pos = first + lax.broadcasted_iota(jnp.int32, (starts.shape[0], rows), 1)
    return ((pos >= starts) & (pos < finish)).astype(F32).astype(BF16)


def pool_own_kernel(table_ref, bytes_ref, starts_ref, finish_ref, sums_ref, member_ref):
    starts, finish = starts_ref[...], finish_ref[...]
    rows = bytes_ref.shape[0]
    rim = rows // 4
    first = table_ref[0] * rows
    total = None
    for part in range(4):
        member = member_of(first + part * rim, rim, starts, finish)
        value = dot(member, bytes_ref[part * rim : (part + 1) * rim, :])
        total = value if total is None else total + value
    sums_ref[...] = total
    member_ref[:, :rim] = member_of(first - rim, rim, starts, finish)
    member_ref[:, rim:] = member_of(first + rows, rim, starts, finish)


def pool_rim_kernel(part, before_ref, after_ref, sums_ref, member_ref, starts_ref, finish_ref, out_ref):
    rim = before_ref.shape[0]
    width = out_ref.shape[1]
    cols = slice(part * width, (part + 1) * width)
    total = sums_ref[:, cols]
    total += dot(member_ref[:, :rim], before_ref[:, cols])
    total += dot(member_ref[:, rim:], after_ref[:, cols])
    out_ref[...] = (total / (finish_ref[...] - starts_ref[...]).astype(F32)).astype(BF16)


def project_kernel(plan, fresh, close, table_ref, gain_ref, q_ref, k_ref, v_ref, *refs):
    refs = list(refs)
    w_refs = [q_ref, k_ref, v_ref]
    x_refs = [refs.pop(0) for _ in plan]
    if fresh:
        sem = refs.pop()
        kept = refs[2:5]
        copies = [pltpu.make_async_copy(a, b, sem.at[i]) for i, (a, b) in enumerate(zip(w_refs, kept))]
        for copy in copies:
            copy.start()
        w_refs = kept
    else:
        old_sum, old_square = refs.pop(0), refs.pop(0)
    depth = x_refs[0].shape[1]
    columns = q_ref.shape[1]
    blocks = [2 * ((table_ref[1] + distance) % 8) + part for distance, part in plan]
    xs = []
    squares = None
    for ref, block in zip(x_refs, blocks):
        values = ref[...].astype(F32)
        square = values * values
        square = square[:, :128] + square[:, 128:]
        squares = square if squares is None else squares + square
        xs.append((values * gain_ref[block]).astype(BF16))
    if not fresh:
        squares = squares + old_square[...]
    if close:
        features, query_scale = close
        inverse = lax.rsqrt(jnp.sum(squares, axis=1, keepdims=True) / features + 1e-05)
    else:
        refs[1][...] = squares
    half = xs[0].shape[0] // 2
    for i, w_ref in enumerate(w_refs):
        cols = slice(i * columns, (i + 1) * columns)
        if fresh:
            copies[i].wait()
        total = None if fresh else old_sum[:, cols]
        for x, block in zip(xs, blocks):
            value = dot(x, w_ref[pl.ds(pl.multiple_of(block * depth, depth), depth), :])
            total = value if total is None else total + value
        if not close:
            refs[0][:, cols] = total
            continue
        total = total * (inverse * query_scale if i == 0 else inverse)
        for part in range(2):
            rows = slice(part * half, (part + 1) * half)
            if i == 0:
                refs[2 * part][...] = total[rows, :].astype(BF16)
            else:
                refs[2 * part + 1][:, (i - 1) * columns : i * columns] = total[rows, :].astype(BF16)


def project(table, pieces, gain, weights, sums=None, close=None):
    height, depth = pieces[0][2].shape
    columns = weights[0].shape[1]
    plan = tuple((distance, part) for distance, part, _ in pieces)
    rest = [x for _, _, x in pieces] + list(sums or ())
    fresh = sums is None
    scratch = []
    if close:
        out_shape = [shape(height // 2, columns), shape(height // 2, 2 * columns)] * 2
    else:
        out_shape = [shape(height, 3 * columns, F32), shape(height, 128, F32)]
    if fresh:
        out_shape += [shape(*w.shape) for w in weights]
        scratch = [pltpu.SemaphoreType.DMA((3,))]
    w_spec = pl.BlockSpec(memory_space=pltpu.HBM) if fresh else whole()
    return pl.pallas_call(
        functools.partial(project_kernel, plan, fresh, close),
        in_specs=[scalars(), whole()] + [w_spec] * 3 + [whole()] * len(rest),
        out_specs=[whole()] * len(out_shape),
        out_shape=out_shape,
        scratch_shapes=scratch,
        compiler_params=params(FIRST_LIMIT if fresh else VMEM_LIMIT),
        cost_estimate=cost(len(plan) * 6 * height * depth * columns, 6 * depth * columns * len(plan)),
        name="project",
    )(table, gain, *weights, *rest)


def attend_kernel(steps, heads, own, fresh, close, table_ref, *refs):
    refs = list(refs)
    count = len(steps)
    q_refs = [refs.pop(0) for _ in range(2)]
    low_ref = refs.pop(0)
    pair_refs = [(refs.pop(0), refs.pop(0)) for _ in range(count)]
    olds = [] if fresh else [refs.pop(0) for _ in range(3)]
    out_refs = [refs.pop(0) for _ in range(2)] if close else []
    top_ref, total_ref, accum_ref = refs
    half = q_refs[0].shape[0]
    width = heads * HEAD_DIM
    if fresh:
        top_ref[...] = jnp.full(top_ref.shape, NEG, F32)
        total_ref[...] = jnp.zeros(total_ref.shape, F32)
        accum_ref[...] = jnp.zeros(accum_ref.shape, F32)
    else:
        for ref, old in zip((top_ref, total_ref, accum_ref), olds):
            ref[...] = old[...]
    here = table_ref[0]
    ones = jnp.ones((half, HEAD_DIM), BF16)

    def tile(slot, qh, block):
        low = low_ref[qh * half : (qh + 1) * half, :]
        rows = slice(qh * half, (qh + 1) * half)
        parts = (0,) if own and qh == 0 else (0, 1)
        allowed = {}
        for kh in parts:
            key_pos = (2 * block + kh) * half + lax.broadcasted_iota(jnp.int32, (half, half), 1)
            allowed[kh] = key_pos >= low
            if own and kh == qh:
                query_pos = (2 * here + qh) * half + lax.broadcasted_iota(jnp.int32, (half, half), 0)
                allowed[kh] = allowed[kh] & (key_pos <= query_pos)
        for head in range(heads):
            cols = slice(head * HEAD_DIM, (head + 1) * HEAD_DIM)
            value_cols = slice(width + head * HEAD_DIM, width + (head + 1) * HEAD_DIM)
            query = q_refs[qh][:, cols]
            scores = {}
            for kh in parts:
                value = lax.dot_general(
                    query,
                    pair_refs[slot][kh][:, cols],
                    (((1,), (1,)), ((), ())),
                    preferred_element_type=F32,
                )
                scores[kh] = jnp.where(allowed[kh], value, NEG)
            best = scores[0] if len(parts) == 1 else jnp.maximum(scores[0], scores[1])
            top = top_ref[rows, cols]
            new_top = jnp.maximum(top, jnp.max(best, axis=1, keepdims=True))
            fade = jnp.exp2(top - new_top)
            update = None
            for kh in parts:
                weights = jnp.exp2(scores[kh] - new_top[:, 0:1]).astype(BF16)
                values = jnp.concatenate([pair_refs[slot][kh][:, value_cols], ones], axis=1)
                value = dot(weights, values)
                update = value if update is None else update + value
            accum_ref[rows, cols] = accum_ref[rows, cols] * fade + update[:, :HEAD_DIM]
            total_ref[rows, cols] = total_ref[rows, cols] * fade + update[:, HEAD_DIM:]
            top_ref[rows, cols] = new_top

    for slot in range(count):
        block = here - steps[slot]
        for qh in range(2):
            if own:
                tile(slot, qh, block)
            else:
                pl.when((block >= 0) & ((block + 1) * 2 * half > table_ref[2 + qh]))(
                    functools.partial(tile, slot, qh, block)
                )
    for qh, ref in enumerate(out_refs):
        rows = slice(qh * half, (qh + 1) * half)
        ref[...] = (accum_ref[rows, :] / total_ref[rows, :]).astype(BF16)


def attend(table, queries, low, pairs, steps, carry=None, close=False):
    rows = low.shape[0]
    half = rows // 2
    width = queries[0].shape[1]
    heads = width // HEAD_DIM
    operands = list(queries) + [low]
    for pair in pairs:
        operands += list(pair)
    operands += list(carry or ())
    scratch = []
    if close:
        out_shape = [shape(half, width)] * 2
        scratch = [pltpu.VMEM((rows, width), F32)] * 3
    else:
        out_shape = [shape(rows, width, F32)] * 3
    fresh = carry is None
    return pl.pallas_call(
        functools.partial(attend_kernel, tuple(steps), heads, fresh, fresh, close),
        in_specs=[scalars()] + [whole()] * len(operands),
        out_specs=[whole()] * len(out_shape),
        out_shape=out_shape,
        scratch_shapes=scratch,
        compiler_params=params(),
        cost_estimate=cost(16 * rows * rows * width * len(pairs), 4 * rows * width),
        name="attend",
    )(table, *operands)


def join_kernel(a_ref, b_ref, out_ref):
    rows = a_ref.shape[0]
    out_ref[:rows, :] = a_ref[...]
    out_ref[rows:, :] = b_ref[...]


def join(a, b):
    return pl.pallas_call(
        join_kernel,
        in_specs=[whole()] * 2,
        out_specs=whole(),
        out_shape=shape(2 * a.shape[0], a.shape[1]),
        compiler_params=params(),
        cost_estimate=cost(0, 8 * a.shape[0] * a.shape[1]),
        name="join",
    )(a, b)


def slice_of(rank):
    return (rank & 1) + 2 * ((rank >> 2) & 1) + 4 * ((rank >> 3) & 1)


def order_kernel(ranks, table_ref, mine_ref, other_ref, out_ref):
    width = mine_ref.shape[1]
    slice_rows = mine_ref.shape[0] // (8 * ranks)
    first_half = table_ref[4] == 0
    mine_at = slice_of(table_ref[0])
    for rank in range(ranks):
        j = mine_at ^ rank
        for k in range(8):
            rows = pl.ds(pl.multiple_of((j * 8 + k) * slice_rows, slice_rows), slice_rows)
            target = slice((k * ranks + rank) * slice_rows, (k * ranks + rank + 1) * slice_rows)
            mine, other = mine_ref[rows, :], other_ref[rows, :]
            out_ref[target, :width] = jnp.where(first_half, mine, other)
            out_ref[target, width:] = jnp.where(first_half, other, mine)


def mix_kernel(plan, fresh, table_ref, w_ref, *refs):
    refs = list(refs)
    out_ref = refs.pop()
    x_refs = [refs.pop(0) for _ in plan]
    place = table_ref[1]
    for part in range(2):
        half, depth = x_refs[0].shape
        rows = slice(part * half, (part + 1) * half)
        total = None if fresh else refs[0][rows, :]
        for (distance, own), x_ref in zip(plan, x_refs):
            if own != part:
                continue
            q = place ^ ((place + distance) % 8)
            k = ((q >> 2) & 1) + 2 * ((q >> 1) & 1) + 4 * (q & 1)
            value = dot(x_ref[...], w_ref[pl.ds(pl.multiple_of(k * depth, depth), depth), :])
            total = value if total is None else total + value
        out_ref[rows, :] = total.astype(out_ref.dtype)


def mix(table, pieces, columns, total=None, dtype=F32):
    half, depth = pieces[0][2].shape
    width = columns.shape[1]
    operands = [columns] + [x for _, _, x in pieces] + ([] if total is None else [total])
    return pl.pallas_call(
        functools.partial(mix_kernel, tuple((d, p) for d, p, _ in pieces), total is None),
        in_specs=[scalars()] + [whole()] * len(operands),
        out_specs=whole(),
        out_shape=shape(2 * half, width, dtype),
        compiler_params=params(),
        cost_estimate=cost(2 * half * depth * width * len(pieces), 2 * half * width),
        name="mix",
    )(table, *operands)


def chips(move):
    pairs = []
    for y in range(SIDE):
        for x in range(SIDE):
            target = move(y, x)
            if target is not None:
                pairs.append((SIDE * y + x, SIDE * target[0] + target[1]))
    return pairs


def per_device(byte_states, patch_spans, doc_lengths, norm_gain, w_query, w_key, w_value, w_out):
    rank = lax.axis_index("seq")
    place = lax.axis_index("tensor")
    seq = lax.axis_size("seq")
    ring = lax.axis_size("tensor")
    byte_rows, depth = byte_states.shape
    rim = byte_rows // 4
    patch_rows = patch_spans.shape[0]
    half = patch_rows // 2
    column = rank % SIDE
    wide = depth // 2
    up = [(i, i + 1) for i in range(seq - 1)]
    down = [(j, i) for i, j in up]

    table = jnp.stack([rank, place]).astype(jnp.int32)

    last, first = byte_states[byte_rows - rim :], byte_states[:rim]
    before = lax.ppermute(last, "seq", up)
    after = lax.ppermute(first, "seq", down)

    slices = 2 * SIDE
    slice_rows = w_out.shape[0] // slices

    def cut(value, bit):
        side = (place // bit) % 2
        wide_half = value.shape[1] // 2
        keep = lax.dynamic_slice_in_dim(value, side * wide_half, wide_half, axis=1)
        give = lax.dynamic_slice_in_dim(value, (1 - side) * wide_half, wide_half, axis=1)
        return keep, give

    def trade(keep, give, bit):
        got = lax.ppermute(give, "tensor", [(i, i ^ bit) for i in range(ring)])
        return jnp.concatenate([keep, got], axis=0)

    columns = lax.dynamic_slice_in_dim(w_out, slice_of(rank) * slice_rows, slice_rows, axis=0)
    for bit in (4, 2):
        columns = trade(*cut(columns, bit), bit)
    keep, give = cut(columns, 1)
    double = lambda value, bit: join(
        value, lax.ppermute(value, "seq", [(i, i ^ bit) for i in range(seq)])
    )

    starts = patch_spans[:, 0:1]
    finish = patch_spans[:, 1:2]
    ends = jnp.cumsum(doc_lengths)
    positions = rank * patch_rows + jnp.arange(patch_rows, dtype=jnp.int32)
    low = jnp.max(jnp.where(ends[None, :] <= positions[:, None], ends[None, :], 0), axis=1)[:, None]
    long_table = jnp.concatenate([table, low[0], low[half], lax.axis_index("dp").astype(jnp.int32)[None]])

    sums, member = pl.pallas_call(
        pool_own_kernel,
        in_specs=[scalars()] + [whole()] * 3,
        out_specs=[whole()] * 2,
        out_shape=[shape(patch_rows, depth, F32), shape(patch_rows, 2 * rim)],
        compiler_params=params(),
        cost_estimate=cost(4 * patch_rows * byte_rows * depth, 2 * byte_rows * depth),
        name="pool_own",
    )(table, byte_states, starts, finish)
    sums, low, long_table, keep, give = lax.optimization_barrier((sums, low, long_table, keep, give))
    columns = trade(keep, give, 1)
    core = lax.axis_index("dp")
    columns = lax.dynamic_slice_in_dim(columns, core * (columns.shape[1] // 2), columns.shape[1] // 2, axis=1)
    pooled = [
        pl.pallas_call(
            functools.partial(pool_rim_kernel, part),
            in_specs=[whole()] * 6,
            out_specs=whole(),
            out_shape=shape(patch_rows, wide),
            compiler_params=params(),
            cost_estimate=cost(4 * patch_rows * rim * wide, 2 * rim * wide),
            name="pool_rim",
        )(before, after, sums, member, starts, finish)
        for part in range(2)
    ]

    right = [(i, (i + 1) % ring) for i in range(ring)]
    left = [(j, i) for i, j in right]
    gain = norm_gain.reshape(2 * ring, 1, wide)
    going = [(x, x) for x in pooled]
    weights = (w_query, w_key, w_value)
    pieces = [(0, part, pooled[part]) for part in range(2)]
    states = []
    for distance in range(1, ring // 2):
        early = () if distance < 3 else (states[distance - 3], columns)
        if early:
            going = [tuple(tie(x, *early) for x in pair) for pair in going]
        going = [
            (lax.ppermute(a, "tensor", right), lax.ppermute(b, "tensor", left)) for a, b in going
        ]
        for part in range(2):
            pieces.append((ring - distance, part, going[part][0]))
            pieces.append((distance, part, going[part][1]))
        if distance == 1:
            first = project(table, pieces, gain, weights)
            states.append(first[:2])
            weights = first[2:]
        elif distance < ring // 2 - 1:
            states.append(project(table, pieces, gain, weights, states[-1]))
        if distance < ring // 2 - 1:
            pieces = []
    last = [
        lax.ppermute(tie(going[0][0], states[-1]), "tensor", right),
        lax.ppermute(tie(going[1][1], states[-1]), "tensor", left),
    ]
    columns = double(tie(columns, states[-1]), 1)
    pieces += [(ring // 2, part, last[part]) for part in range(2)]
    close = (float(depth * ring), LOG2_E / HEAD_DIM**0.5)
    done = project(table, pieces, gain, weights, states[-1], close)
    queries, pairs = done[0::2], done[1::2]

    lower = chips(lambda y, x: (y + 1, x) if y + 1 < SIDE else None)
    plus = chips(lambda y, x: (y, (x + 1) % SIDE))
    minus = chips(lambda y, x: (y, (x - 1) % SIDE))
    two = chips(lambda y, x: (y, (x + 2) % SIDE))
    slots = {4: [], 1: [], 3: [], 2: []}
    for own in pairs:
        above = lax.ppermute(own, "seq", lower)
        slots[4].append(above)
        slots[1].append(lax.ppermute(jnp.where(column == SIDE - 1, above, own), "seq", plus))
        slots[3].append(lax.ppermute(jnp.where(column == 0, own, above), "seq", minus))
        slots[2].append(lax.ppermute(jnp.where(column < 2, own, above), "seq", two))

    carry = attend(long_table, queries, low, [pairs], [0])
    columns = double(tie(columns, carry[0]), 4)
    columns = double(tie(columns, slots[3][0]), 8)
    for steps in ((4,), (1, 3), (2,)):
        carry = attend(
            long_table, queries, low, [slots[n] for n in steps], steps, carry, steps == (2,)
        )
    attended = carry

    going = [(x, x) for x in attended]
    pieces = [(0, part, attended[part]) for part in range(2)]
    for distance in range(1, ring // 2):
        going = [
            (lax.ppermute(a, "tensor", right), lax.ppermute(b, "tensor", left)) for a, b in going
        ]
        if distance == 1:
            columns = tie(columns, attended[1])
            others = lax.ppermute(columns, "dp", [(0, 1), (1, 0)])
        fresh = []
        for part in range(2):
            fresh.append((ring - distance, part, going[part][0]))
            fresh.append((distance, part, going[part][1]))
        if distance < ring // 2 - 1:
            pieces += fresh
    columns = pl.pallas_call(
        functools.partial(order_kernel, slices),
        in_specs=[scalars()] + [whole()] * 2,
        out_specs=whole(),
        out_shape=shape(columns.shape[0], 2 * columns.shape[1]),
        compiler_params=params(),
        cost_estimate=cost(0, 8 * columns.shape[0] * columns.shape[1]),
        name="order",
    )(long_table, columns, others)
    total = mix(long_table, pieces, columns)
    fresh += [
        (ring // 2, 0, lax.ppermute(tie(going[0][0], total), "tensor", right)),
        (ring // 2, 1, lax.ppermute(tie(going[1][1], total), "tensor", left)),
    ]
    return mix(long_table, fresh, columns, total, BF16)


def solution(mesh):
    in_specs = (
        P(("dp", "seq"), "tensor"),
        P(("dp", "seq"), None),
        P("dp"),
        P(),
        P(None, "tensor"),
        P(None, "tensor"),
        P(None, "tensor"),
        P("tensor", None),
    )
    out_specs = P(("dp", "seq"), "tensor")
    return jax.shard_map(
        per_device, mesh=mesh, in_specs=in_specs, out_specs=out_specs, check_vma=False
    )
```
